128 devices in a mesh: batch: 4 (over z), proto: 32 (over x, y, core).
Axes of the slice: x: 4, y: 4, z: 4, core: 2. Of those that a mesh axis runs over, the one named last changes fastest.
Arguments:
- features: float32 [8192, 256], P(('batch', 'proto')), may hold values from -100 to 100, as said below
- prototypes: bfloat16 [256, 65536], P(None, ('proto', 'batch')), may hold values from -2 to 2, as said below
Outputs:
- targets: float32 [8192, 65536], P('batch', 'proto')
The draws below stay inside these ranges and needn't reach their ends.
Inputs may be any that keep to these rules, and one draw needn't show every extreme that they name: `features`: real values, bounded by 100 in magnitude. `prototypes`: real values.
All inputs are finite; a program needn't handle non-finite values.
Results may differ from the reference program's by a relative error of at most 0.0026.
Values may be sent and summed in bfloat16 or wider, within the bound.
A program may use at most 64 MiB of HBM per device.

```python
import jax
import jax.numpy as jnp
from jax import lax

BOTTLE = 256
PROTOS = 65536
ROWS = 8192
ITERS = 3


def cluster_centres(key):
    clusters = max(4, PROTOS // 256)
    centre_key = jax.random.fold_in(key, 5)
    return jnp.clip(jax.random.normal(centre_key, (clusters, BOTTLE), jnp.float32), -4.0, 4.0)


def draw_prototypes(key, part):
    centres = cluster_centres(key)
    key = jax.random.fold_in(key, 23)
    assign_key, noise_key = jax.random.split(key, 2)
    clusters = centres.shape[0]
    assign = jnp.sort(jax.random.randint(assign_key, (PROTOS,), 0, clusters))
    noise = jnp.clip(jax.random.normal(noise_key, (PROTOS, BOTTLE), jnp.float32), -4.0, 4.0)
    column_count = centres[assign] + noise
    return (column_count.T * BOTTLE ** (-0.5)).astype(jnp.bfloat16)


def draw_features(key, part):
    centres = cluster_centres(key)
    key = jax.random.fold_in(key, 11)
    first_key, second_key, third_key, sharp_key, noise_key = jax.random.split(key, 5)
    clusters = centres.shape[0]
    lowest = jnp.minimum(jax.random.randint(first_key, (ROWS,), 0, clusters), jax.random.randint(second_key, (ROWS,), 0, clusters))
    assign = jnp.sort(jnp.minimum(lowest, jax.random.randint(third_key, (ROWS,), 0, clusters)))
    sharpness = jax.random.uniform(sharp_key, (ROWS, 1), jnp.float32, 0.0, 2.5)
    noise = jnp.clip(jax.random.normal(noise_key, (ROWS, BOTTLE), jnp.float32), -4.0, 4.0)
    score_values = sharpness * centres[assign] + noise
    return jnp.clip(score_values, -100.0, 100.0).astype(jnp.float32)


def setup_inputs(seed: int = 0) -> dict:
    streams_of = jax.random.split(jax.random.key(seed), 3)
    features = draw_features(jax.random.fold_in(streams_of[2], 71), 0)
    prototypes = draw_prototypes(jax.random.fold_in(streams_of[2], 71), 0)
    return dict(features=features, prototypes=prototypes)


eps = 1e-06
sharpening_divisor = 0.07

def reference(features, prototypes):
    score_values = features.astype(jnp.float32)
    equalized_logits = (score_values * lax.rsqrt(lax.optimization_barrier(jnp.sum(score_values * score_values, axis=1, keepdims=True)) + eps)).astype(jnp.bfloat16)
    weights = prototypes.astype(jnp.float32)
    normalised_prototype_mass = (weights * lax.rsqrt(lax.optimization_barrier(jnp.sum(weights * weights, axis=0, keepdims=True)) + eps)).astype(jnp.bfloat16)
    exponentiated_logits = jnp.exp(jnp.dot(equalized_logits, normalised_prototype_mass, preferred_element_type=jnp.float32) / sharpening_divisor)
    row_scale = jnp.ones((ROWS,), jnp.float32)
    col_scale = jnp.ones((PROTOS,), jnp.float32)
    for sweep in range(ITERS):
        col_scale = 1.0 / (PROTOS * lax.optimization_barrier(jnp.sum(exponentiated_logits * row_scale[:, None], axis=0)))
        row_scale = 1.0 / (ROWS * lax.optimization_barrier(jnp.sum(exponentiated_logits * col_scale[None, :], axis=1)))
    return exponentiated_logits * row_scale[:, None] * col_scale[None, :] * (ROWS * PROTOS)
```

```python
import functools

import jax
import jax.numpy as jnp
from jax import lax
from jax.experimental import pallas as pl
from jax.experimental.pallas import tpu as pltpu
from jax.sharding import PartitionSpec as P

ITERS = 3
PROTOS = 65536
ROWS = 8192
eps = 1e-06
sharpening_divisor = 0.07
LOG2E = 1.4426950408889634
EXP2_SCALE = LOG2E / sharpening_divisor

NZ = 4
NP = 32
N_ROWS = ROWS // NZ
N_COLS = PROTOS // NP
WIDTH = 256
QCOLS = N_COLS // NZ
FROWS = N_ROWS // NP
BLOCK = 256
HP = 4
HROWS = N_ROWS // HP
PCHUNK = WIDTH // 4

MESH = pl.DeviceIdType.MESH
SIBLING_ORDER = sorted(
    ((dx, dy) for dx in range(4) for dy in range(4) if dx or dy),
    key=lambda d: min(d[0], 4 - d[0]) + min(d[1], 4 - d[1]),
)


def two_parts(vector):
    high = vector.astype(jnp.bfloat16).astype(jnp.float32)
    low = vector - high
    row = lax.broadcasted_iota(jnp.int32, (16, vector.shape[1]), 0)
    return jnp.where(row == 0, high, jnp.where(row == 1, low, 0.0)).astype(jnp.bfloat16)


def matvec(parts, matrix):
    return jnp.dot(parts, matrix, preferred_element_type=jnp.float32)


def join(product):
    return product[0:1] + product[1:2]


def balance_kernel(
    feat, proto, f_out, p_out, r_out, c_out,
    fb, ft, pb, pt, e, et, el, zs, zr, ps, pr,
    s_right, s_left, s_fwd, r_left, r_right, r_far,
    s_feat, r_feat, s_sib, r_sib, s_z, r_z, s_p, r_p, s_out,
):
    z = lax.axis_index("batch")
    p = lax.axis_index("proto")
    x, y, core = p // 8, (p // 2) % 4, p % 2
    left, right, far = (z + 3) % 4, (z + 1) % 4, (z + 2) % 4

    def plane(dx, dy, dc):
        return ((x + dx) % 4) * 8 + ((y + dy) % 4) * 2 + (core + dc) % 2

    def plane_of(j):
        return plane(j // 8, (j // 2) % 4, j % 2)

    barrier = pltpu.get_barrier_semaphore()

    def greet(j, carry):
        pl.semaphore_signal(barrier, inc=1, device_id=(z, plane_of(j)), device_id_type=MESH)
        return carry

    for dz in range(1, NZ):
        pl.semaphore_signal(barrier, inc=1, device_id=((z + dz) % 4, p), device_id_type=MESH)
    lax.fori_loop(1, NP, greet, 0)

    def rows_of(owner):
        return pl.ds(pl.multiple_of(owner * FROWS, FROWS), FROWS)

    raw = proto[...].astype(jnp.float32)
    pb[z] = (raw * lax.rsqrt(jnp.sum(raw * raw, axis=0, keepdims=True) + eps)).astype(jnp.bfloat16)
    raw = feat[...]
    fb[rows_of(p), :] = (
        raw * lax.rsqrt(jnp.sum(raw * raw, axis=1, keepdims=True) + eps)
    ).astype(jnp.bfloat16)

    pl.semaphore_wait(barrier, NP - 1 + NZ - 1)

    def send(src, dst, send_sem, recv_sem, target):
        copy = pltpu.make_async_remote_copy(
            src_ref=src, dst_ref=dst, send_sem=send_sem, recv_sem=recv_sem,
            device_id=target, device_id_type=MESH,
        )
        copy.start()

    def arrived(ref, sem):
        pltpu.make_async_remote_copy(
            src_ref=ref, dst_ref=ref, send_sem=sem, recv_sem=sem,
            device_id=(right, p), device_id_type=MESH,
        ).wait_recv()

    def sent(ref, sem):
        pltpu.make_async_remote_copy(
            src_ref=ref, dst_ref=ref, send_sem=sem, recv_sem=sem,
            device_id=(right, p), device_id_type=MESH,
        ).wait_send()

    def chunk(owner, k):
        return pb.at[owner, pl.ds(k * PCHUNK, PCHUNK), :]

    for k in range(4):
        kr, kl = k, (k + 2) % 4
        send(chunk(z, kr), chunk(z, kr), s_right.at[kr], r_left.at[kr], (right, p))
        send(chunk(z, kl), chunk(z, kl), s_left.at[kl], r_right.at[kl], (left, p))

    sibling = plane(0, 0, 1)
    mine = fb.at[rows_of(p), :]
    for n, (dx, dy) in reversed(list(enumerate(SIBLING_ORDER))):
        send(mine, mine, s_feat.at[n], r_feat.at[n], (z, plane(dx, dy, 0)))
    send(mine, mine, s_sib.at[15], r_sib.at[15], (z, sibling))

    def pass_feature(n):
        dx, dy = SIBLING_ORDER[n]
        block = fb.at[rows_of(plane(4 - dx, 4 - dy, 0)), :]
        arrived(block, r_feat.at[n])
        send(block, block, s_sib.at[n], r_sib.at[n], (z, sibling))

    def pass_proto(k):
        arrived(chunk(left, k), r_left.at[k])
        send(chunk(left, k), chunk(left, k), s_fwd.at[k], r_far.at[k], (right, p))
        arrived(chunk(right, k + 2), r_right.at[k + 2])
        send(chunk(right, k + 2), chunk(right, k + 2), s_fwd.at[k + 2], r_far.at[k + 2], (left, p))

    for n in range(4):
        pass_feature(n)
    pass_proto(0)
    for n in range(4, 10):
        pass_feature(n)
    pass_proto(1)
    for n in range(10, 15):
        pass_feature(n)
    for n in range(15):
        dx, dy = SIBLING_ORDER[n]
        arrived(fb.at[rows_of(plane(4 - dx, 4 - dy, 1)), :], r_sib.at[n])
    arrived(fb.at[rows_of(sibling), :], r_sib.at[15])

    def send_columns(it, q, total):
        zs[it, q] = total
        for dz in range(1, NZ):
            send(zs.at[it, q], zr.at[it, q, dz], s_z.at[it, q], r_z.at[it, q], ((z + dz) % 4, p))

    def score_block(q):
        def visit(i, total):
            rows = pl.ds(pl.multiple_of(i * BLOCK, BLOCK), BLOCK)
            s = jnp.dot(fb[rows, :], pb[q], preferred_element_type=jnp.float32)
            t = jnp.exp2(s * EXP2_SCALE)
            e[q, rows, :] = t.astype(jnp.bfloat16)
            return total + jnp.sum(t.reshape(BLOCK // 8, 8, QCOLS), axis=0)

        total = lax.fori_loop(0, N_ROWS // BLOCK, visit, jnp.zeros((8, QCOLS), jnp.float32))
        send_columns(0, q, jnp.sum(total, axis=0, keepdims=True))

    def turn_features():
        def visit(i, carry):
            rows = pl.ds(pl.multiple_of(i * BLOCK, BLOCK), BLOCK)
            ft[:, rows] = fb[rows, :].T
            return carry

        lax.fori_loop(0, N_ROWS // BLOCK, visit, 0)

    def score_turned(q, low):
        if not low:
            pt[q] = pb[q].T

        def visit(i, carry):
            cols = pl.ds(pl.multiple_of(i * BLOCK, BLOCK), BLOCK)
            s = jnp.dot(pt[q, cols, :], ft[...], preferred_element_type=jnp.float32)
            t = jnp.exp2(s * EXP2_SCALE)
            high = t.astype(jnp.bfloat16)
            if low:
                el[q, cols, :] = (t - high.astype(jnp.float32)).astype(jnp.bfloat16)
            else:
                et[q, cols, :] = high
            return carry

        lax.fori_loop(0, QCOLS // BLOCK, visit, 0)

    score_block(z)
    for k in (2, 3):
        arrived(chunk(left, k), r_left.at[k])
    score_block(left)
    for k in (0, 1):
        arrived(chunk(right, k), r_right.at[k])
    score_block(right)
    turn_features()
    score_turned(z, False)
    for k in range(4):
        arrived(chunk(far, k), r_far.at[k])
    score_block(far)

    f_copy = pltpu.make_async_copy(fb, f_out, s_out.at[0])
    p_copy = pltpu.make_async_copy(pb, p_out, s_out.at[1])
    f_copy.start()
    p_copy.start()
    score_turned(left, False)
    score_turned(right, False)
    score_turned(far, False)

    def send_rows(it, h, total):
        ps[it, h] = total

        def one(j, carry):
            send(ps.at[it, h], pr.at[it, h, j], s_p.at[it, h], r_p.at[it, h], (z, plane_of(j)))
            return carry

        lax.fori_loop(1, NP, one, 0)

    for it in range(ITERS):
        last = it == ITERS - 1
        if it > 0:
            totals = [jnp.zeros((16, QCOLS), jnp.float32)] * NZ
            for h in range(HP):
                arrived(pr.at[it - 1, h, pl.ds(1, NP - 1)], r_p.at[it - 1, h])
                row_sum = ps[it - 1, h] + jnp.sum(pr[it - 1, h, 1:NP], axis=0)
                parts = two_parts(1.0 / (ROWS * row_sum))
                for q in range(NZ):
                    totals[q] = totals[q] + matvec(parts, e[q, h * HROWS:(h + 1) * HROWS, :])
                    if h == HP - 1:
                        send_columns(it, q, join(totals[q]))
        totals = [jnp.zeros((16, HROWS), jnp.float32)] * HP
        for q in range(NZ):
            arrived(zr.at[it, q, pl.ds(1, NZ - 1)], r_z.at[it, q])
            col_sum = zs[it, q] + jnp.sum(zr[it, q, 1:NZ], axis=0)
            col_scale = 1.0 / (PROTOS * col_sum)
            if last:
                c_out[q] = col_scale
            parts = two_parts(col_scale)
            for h in range(HP):
                rows = slice(h * HROWS, (h + 1) * HROWS)
                totals[h] = totals[h] + matvec(parts, et[q, :, rows])
                if last:
                    totals[h] = totals[h] + matvec(parts, el[q, :, rows])
                if q == NZ - 1:
                    send_rows(it, h, join(totals[h]))
        if it == 0:
            for q in range(NZ):
                score_turned(q, True)

    for h in range(HP):
        arrived(pr.at[ITERS - 1, h, pl.ds(1, NP - 1)], r_p.at[ITERS - 1, h])
        row_sum = ps[ITERS - 1, h] + jnp.sum(pr[ITERS - 1, h, 1:NP], axis=0)
        r_out[:, h * HROWS:(h + 1) * HROWS] = 1.0 / (ROWS * row_sum)

    for k in range(4):
        sent(chunk(z, k), s_right.at[k])
        sent(chunk(z, k), s_left.at[k])
        sent(chunk(z, k), s_fwd.at[k])
    for n in range(15):
        sent(mine, s_feat.at[n])
        sent(mine, s_sib.at[n])
    sent(mine, s_sib.at[15])
    for it in range(ITERS):
        for q in range(NZ):
            sent(zr.at[it, q, pl.ds(1, NZ - 1)], s_z.at[it, q])
        for h in range(HP):
            sent(pr.at[it, h, pl.ds(1, NP - 1)], s_p.at[it, h])
    f_copy.wait()
    p_copy.wait()


def balance(features, prototypes):
    f32, bf16 = jnp.float32, jnp.bfloat16
    vmem = pl.BlockSpec(memory_space=pltpu.VMEM)
    anywhere = pl.BlockSpec(memory_space=pl.ANY)
    dma = pltpu.SemaphoreType.DMA
    return pl.pallas_call(
        balance_kernel,
        out_shape=(
            jax.ShapeDtypeStruct((N_ROWS, WIDTH), bf16),
            jax.ShapeDtypeStruct((NZ, WIDTH, QCOLS), bf16),
            jax.ShapeDtypeStruct((1, N_ROWS), f32),
            jax.ShapeDtypeStruct((NZ, 1, QCOLS), f32),
        ),
        in_specs=[vmem, vmem],
        out_specs=(anywhere, anywhere, vmem, vmem),
        scratch_shapes=[
            pltpu.VMEM((N_ROWS, WIDTH), bf16),
            pltpu.VMEM((WIDTH, N_ROWS), bf16),
            pltpu.VMEM((NZ, WIDTH, QCOLS), bf16),
            pltpu.VMEM((NZ, QCOLS, WIDTH), bf16),
            pltpu.VMEM((NZ, N_ROWS, QCOLS), bf16),
            pltpu.VMEM((NZ, QCOLS, N_ROWS), bf16),
            pltpu.VMEM((NZ, QCOLS, N_ROWS), bf16),
            pltpu.VMEM((ITERS, NZ, 1, QCOLS), f32),
            pltpu.VMEM((ITERS, NZ, NZ, 1, QCOLS), f32),
            pltpu.VMEM((ITERS, HP, 1, HROWS), f32),
            pltpu.VMEM((ITERS, HP, NP, 1, HROWS), f32),
            dma((4,)), dma((4,)), dma((4,)), dma((4,)), dma((4,)), dma((4,)),
            dma((15,)), dma((15,)), dma((16,)), dma((16,)),
            dma((ITERS, NZ)), dma((ITERS, NZ)), dma((ITERS, HP)), dma((ITERS, HP)),
            dma((2,)),
        ],
        compiler_params=pltpu.CompilerParams(
            collective_id=0, has_side_effects=True, vmem_limit_bytes=44 * 2**20
        ),
        cost_estimate=pl.CostEstimate(
            flops=6 * N_ROWS * N_COLS * WIDTH, bytes_accessed=4 * 2**20, transcendentals=3 * N_ROWS * N_COLS
        ),
        name="balance",
    )(features, prototypes)


def write_kernel(f, p, r, c, out, buf, rc, sem):
    steps = N_ROWS // BLOCK
    rc[...] = jnp.broadcast_to(r[...], (8, N_ROWS)).T[:, 0:1]
    scale = [c[q] * float(ROWS * PROTOS) for q in range(NZ)]

    def store(i):
        return pltpu.make_async_copy(
            buf.at[i], out.at[pl.ds(pl.multiple_of(i * BLOCK, BLOCK), BLOCK), :], sem.at[i]
        )

    def visit(i, carry):
        rows = pl.ds(pl.multiple_of(i * BLOCK, BLOCK), BLOCK)
        for q in range(NZ):
            s = jnp.dot(f[rows, :], p[q], preferred_element_type=jnp.float32)
            buf[i, :, q * QCOLS:(q + 1) * QCOLS] = jnp.exp2(s * EXP2_SCALE) * rc[rows, :] * scale[q]
        store(i).start()
        return carry

    lax.fori_loop(0, steps, visit, 0)
    for i in range(steps):
        store(i).wait()


def write(f, p, r, c):
    vmem = pl.BlockSpec(memory_space=pltpu.VMEM)
    return pl.pallas_call(
        write_kernel,
        out_shape=jax.ShapeDtypeStruct((N_ROWS, N_COLS), jnp.float32),
        in_specs=[vmem] * 4,
        out_specs=pl.BlockSpec(memory_space=pl.ANY),
        scratch_shapes=[
            pltpu.VMEM((N_ROWS // BLOCK, BLOCK, N_COLS), jnp.float32),
            pltpu.VMEM((N_ROWS, 1), jnp.float32),
            pltpu.SemaphoreType.DMA((N_ROWS // BLOCK,)),
        ],
        compiler_params=pltpu.CompilerParams(vmem_limit_bytes=40 * 2**20),
        cost_estimate=pl.CostEstimate(
            flops=2 * N_ROWS * N_COLS * WIDTH, bytes_accessed=18 * 2**20, transcendentals=N_ROWS * N_COLS
        ),
        name="write",
    )(f, p, r, c)


def body(features, prototypes):
    return write(*balance(features, prototypes))


def solution(mesh):
    in_specs = (P(("batch", "proto"), None), P(None, ("proto", "batch")))
    out_specs = P("batch", "proto")
    return jax.shard_map(body, mesh=mesh, in_specs=in_specs, out_specs=out_specs, check_vma=False)
```

```python
import functools

import jax
import jax.numpy as jnp
from jax import lax
from jax.experimental import pallas as pl
from jax.experimental.pallas import tpu as pltpu
from jax.sharding import PartitionSpec as P

ITERS = 3
PROTOS = 65536
ROWS = 8192
eps = 1e-06
sharpening_divisor = 0.07
LOG2E = 1.4426950408889634
EXP2_SCALE = LOG2E / sharpening_divisor

NZ = 4
NP = 32
N_ROWS = ROWS // NZ
N_COLS = PROTOS // NP
WIDTH = 256
QCOLS = N_COLS // NZ
FROWS = N_ROWS // NP
BLOCK = 256
HALVES = 2
HALF = N_ROWS // HALVES
TILES = HALF // 128
PCHUNK = WIDTH // 4
SLAB = N_ROWS // 4

MESH = pl.DeviceIdType.MESH


def hops(d):
    return sum(min(v, 4 - v) for v in d[:2])


CHIPS = sorted(((dx, dy) for dx in range(4) for dy in range(4) if dx or dy), key=hops, reverse=True)
PEERS = sorted(
    ((dx, dy, dc) for dx in range(4) for dy in range(4) for dc in range(2) if dx or dy or dc),
    key=hops, reverse=True,
)


def operand(dense):
    high = dense.astype(jnp.bfloat16).astype(jnp.float32)
    low = dense - high
    tiles = [
        jnp.concatenate(
            [jnp.broadcast_to(high[i:i + 1], (8, 128)), jnp.broadcast_to(low[i:i + 1], (8, 128))], axis=0
        ).astype(jnp.bfloat16)
        for i in range(TILES)
    ]
    return jnp.concatenate(tiles, axis=1)


def matvec(parts, matrix):
    return jnp.dot(parts, matrix, preferred_element_type=jnp.float32)


def dense_rows(wide):
    row = lax.broadcasted_iota(jnp.int32, (8, 128), 0)
    out = wide[:, 0:128]
    for i in range(1, TILES):
        out = jnp.where(row == i, wide[:, i * 128:(i + 1) * 128], out)
    return out


def join(product):
    return dense_rows(product[0:8] + product[8:16])


def balance_kernel(
    feat_hbm, proto_hbm, f_out, p_out, r_out, c_out,
    feat, proto, fb, ft, pb, pt, e, et, el, col, zs, zr, ps, pr,
    s_in, s_right, s_left, s_fwd, r_left, r_right, r_far,
    s_feat, r_feat, s_sib, r_sib, s_z, r_z, s_p, r_p, s_out,
):
    z = lax.axis_index("batch")
    p = lax.axis_index("proto")
    x, y, core = p // 8, (p // 2) % 4, p % 2
    at_x = [((x + d) % 4) * 8 for d in range(4)]
    at_y = [((y + d) % 4) * 2 for d in range(4)]
    at_core = [core, 1 - core]
    at_z = [(z + d) % 4 for d in range(4)]
    right, far, left = at_z[1], at_z[2], at_z[3]

    def plane(dx, dy, dc):
        return at_x[dx % 4] + at_y[dy % 4] + at_core[dc]

    proto_in = pltpu.make_async_copy(proto_hbm, proto, s_in.at[0])
    feat_in = pltpu.make_async_copy(feat_hbm, feat, s_in.at[1])
    proto_in.start()
    feat_in.start()

    barrier = pltpu.get_barrier_semaphore()
    for d in PEERS:
        pl.semaphore_signal(barrier, inc=1, device_id=(z, plane(*d)), device_id_type=MESH)
    for dz in range(1, NZ):
        pl.semaphore_signal(barrier, inc=1, device_id=(at_z[dz], p), device_id_type=MESH)

    def rows_of(owner):
        return pl.ds(pl.multiple_of(owner * FROWS, FROWS), FROWS)

    proto_in.wait()
    raw = proto[...].astype(jnp.float32)
    pb[z] = (raw * lax.rsqrt(jnp.sum(raw * raw, axis=0, keepdims=True) + eps)).astype(jnp.bfloat16)
    feat_in.wait()
    raw = feat[...]
    fb[rows_of(p), :] = (
        raw * lax.rsqrt(jnp.sum(raw * raw, axis=1, keepdims=True) + eps)
    ).astype(jnp.bfloat16)
    col[...] = jnp.zeros_like(col)
    zs[0] = jnp.zeros((HALVES, 8, 128), jnp.float32)

    pl.semaphore_wait(barrier, NP - 1 + NZ - 1)

    def send(src, dst, send_sem, recv_sem, target):
        pltpu.make_async_remote_copy(
            src_ref=src, dst_ref=dst, send_sem=send_sem, recv_sem=recv_sem,
            device_id=target, device_id_type=MESH,
        ).start()

    def arrived(ref, sem):
        pltpu.make_async_remote_copy(
            src_ref=ref, dst_ref=ref, send_sem=sem, recv_sem=sem,
            device_id=(right, p), device_id_type=MESH,
        ).wait_recv()

    def sent(ref, sem):
        pltpu.make_async_remote_copy(
            src_ref=ref, dst_ref=ref, send_sem=sem, recv_sem=sem,
            device_id=(right, p), device_id_type=MESH,
        ).wait_send()

    def chunk(owner, k):
        return pb.at[owner, pl.ds(k * PCHUNK, PCHUNK), :]

    for k in range(4):
        kr, kl = k, (k + 2) % 4
        send(chunk(z, kr), chunk(z, kr), s_right.at[kr], r_left.at[kr], (right, p))
        send(chunk(z, kl), chunk(z, kl), s_left.at[kl], r_right.at[kl], (left, p))

    sibling = plane(0, 0, 1)
    mine = fb.at[rows_of(p), :]
    for n, (dx, dy) in enumerate(CHIPS):
        send(mine, mine, s_feat.at[n], r_feat.at[n], (z, plane(dx, dy, 0)))
    send(mine, mine, s_sib.at[15], r_sib.at[15], (z, sibling))

    def pass_features(slab):
        for n, (dx, dy) in enumerate(CHIPS):
            if dx == slab:
                block = fb.at[rows_of(plane(4 - dx, 4 - dy, 0)), :]
                arrived(block, r_feat.at[n])
                send(block, block, s_sib.at[n], r_sib.at[n], (z, sibling))

    def pass_proto(k):
        arrived(chunk(left, k), r_left.at[k])
        send(chunk(left, k), chunk(left, k), s_fwd.at[k], r_far.at[k], (right, p))
        arrived(chunk(right, k + 2), r_right.at[k + 2])
        send(chunk(right, k + 2), chunk(right, k + 2), s_fwd.at[k + 2], r_far.at[k + 2], (left, p))

    def wait_slab(slab):
        for n, (dx, dy) in enumerate(CHIPS):
            if dx == slab:
                arrived(fb.at[rows_of(plane(4 - dx, 4 - dy, 1)), :], r_sib.at[n])
        if slab == 0:
            arrived(fb.at[rows_of(sibling), :], r_sib.at[15])

    def score_rows(q, start):
        rows = pl.ds(pl.multiple_of(start, BLOCK), BLOCK)
        s = jnp.dot(fb[rows, :], pb[q], preferred_element_type=jnp.float32)
        t = jnp.exp2(s * EXP2_SCALE)
        e[q, rows, :] = t.astype(jnp.bfloat16)
        col[q] += jnp.sum(t.reshape(BLOCK // 8, 8, QCOLS), axis=0)

    def score_slab(slab):
        start = at_x[(4 - slab) % 4] * (SLAB // 8)

        def visit(i, carry):
            score_rows(z, start + i * BLOCK)
            return carry

        lax.fori_loop(0, SLAB // BLOCK, visit, 0)

    def score_block(q):
        def visit(i, carry):
            score_rows(q, i * BLOCK)
            return carry

        lax.fori_loop(0, N_ROWS // BLOCK, visit, 0)

    def finish_block(q):
        total = jnp.sum(col[q], axis=0, keepdims=True)
        row = lax.broadcasted_iota(jnp.int32, (8, 128), 0)
        out = zs[0, q // 2]
        for i in range(QCOLS // 128):
            out = jnp.where(row == (q % 2) * 4 + i, total[:, i * 128:(i + 1) * 128], out)
        zs[0, q // 2] = out

    def turn_features():
        def visit(i, carry):
            rows = pl.ds(pl.multiple_of(i * BLOCK, BLOCK), BLOCK)
            ft[:, rows] = fb[rows, :].T
            return carry

        lax.fori_loop(0, N_ROWS // BLOCK, visit, 0)

    def score_turned(q, low):
        if not low:
            pt[q] = pb[q].T

        def visit(i, carry):
            cols = pl.ds(pl.multiple_of(i * BLOCK, BLOCK), BLOCK)
            s = jnp.dot(pt[q, cols, :], ft[...], preferred_element_type=jnp.float32)
            t = jnp.exp2(s * EXP2_SCALE)
            high = t.astype(jnp.bfloat16)
            if low:
                el[q, cols, :] = (t - high.astype(jnp.float32)).astype(jnp.bfloat16)
            else:
                et[q, cols, :] = high
            return carry

        lax.fori_loop(0, QCOLS // BLOCK, visit, 0)

    pass_features(0)
    pass_proto(0)
    pass_features(1)
    pass_proto(1)
    pass_features(3)
    wait_slab(0)
    score_slab(0)
    wait_slab(1)
    score_slab(1)
    pass_features(2)
    wait_slab(3)
    score_slab(3)
    wait_slab(2)
    score_slab(2)
    finish_block(z)
    for k in (2, 3):
        arrived(chunk(left, k), r_left.at[k])
    score_block(left)
    finish_block(left)
    for k in (0, 1):
        arrived(chunk(right, k), r_right.at[k])
    score_block(right)
    finish_block(right)
    for k in range(4):
        arrived(chunk(far, k), r_far.at[k])
    score_block(far)
    finish_block(far)

    def send_columns(it, g):
        for dz in (2, 1, 3):
            send(zs.at[it, g], zr.at[it, g, dz], s_z.at[it, g], r_z.at[it, g], (at_z[dz], p))

    def send_rows(it, h):
        for j, d in enumerate(PEERS):
            send(ps.at[it, h], pr.at[it, h, j], s_p.at[it, h], r_p.at[it, h], (z, plane(*d)))

    for g in range(HALVES):
        send_columns(0, g)

    f_copy = pltpu.make_async_copy(fb, f_out, s_out.at[0])
    p_copy = pltpu.make_async_copy(pb, p_out, s_out.at[1])
    f_copy.start()
    p_copy.start()
    turn_features()
    for q in (z, left, right, far):
        score_turned(q, False)

    def row_scale(it, h):
        arrived(pr.at[it, h], r_p.at[it, h])
        return 1.0 / (ROWS * (ps[it, h] + jnp.sum(pr[it, h], axis=0)))

    for it in range(ITERS):
        last = it == ITERS - 1
        if it > 0:
            totals = [jnp.zeros((16, QCOLS), jnp.float32)] * NZ
            for h in range(HALVES):
                parts = operand(row_scale(it - 1, h))
                for q in range(NZ):
                    totals[q] = totals[q] + matvec(parts, e[q, h * HALF:(h + 1) * HALF, :])
                    if h == HALVES - 1 and q % 2:
                        zs[it, q // 2] = join(jnp.concatenate(totals[q - 1:q + 1], axis=1))
                        send_columns(it, q // 2)
        totals = [jnp.zeros((16, HALF), jnp.float32)] * HALVES
        for g in range(HALVES):
            arrived(zr.at[it, g, pl.ds(1, NZ - 1)], r_z.at[it, g])
            col_scale = 1.0 / (PROTOS * (zs[it, g] + jnp.sum(zr[it, g, 1:NZ], axis=0)))
            if last:
                c_out[g] = col_scale
            parts = operand(col_scale)
            for h in range(HALVES):
                rows = slice(h * HALF, (h + 1) * HALF)
                for q in (2 * g, 2 * g + 1):
                    part = parts[:, (q - 2 * g) * QCOLS:(q - 2 * g + 1) * QCOLS]
                    totals[h] = totals[h] + matvec(part, et[q, :, rows])
                    if last:
                        totals[h] = totals[h] + matvec(part, el[q, :, rows])
                if g == HALVES - 1:
                    ps[it, h] = join(totals[h])
                    send_rows(it, h)
        if it == 0:
            for q in range(NZ):
                score_turned(q, True)

    for h in range(HALVES):
        r_out[h] = row_scale(ITERS - 1, h)

    for k in range(4):
        sent(chunk(z, k), s_right.at[k])
        sent(chunk(z, k), s_left.at[k])
        sent(chunk(z, k), s_fwd.at[k])
    for n in range(15):
        sent(mine, s_feat.at[n])
        sent(mine, s_sib.at[n])
    sent(mine, s_sib.at[15])
    for it in range(ITERS):
        for h in range(HALVES):
            sent(zr.at[it, h, pl.ds(1, NZ - 1)], s_z.at[it, h])
            sent(pr.at[it, h], s_p.at[it, h])
    f_copy.wait()
    p_copy.wait()


def balance(features, prototypes):
    f32, bf16 = jnp.float32, jnp.bfloat16
    vmem = pl.BlockSpec(memory_space=pltpu.VMEM)
    anywhere = pl.BlockSpec(memory_space=pl.ANY)
    hbm = pl.BlockSpec(memory_space=pltpu.HBM)
    dma = pltpu.SemaphoreType.DMA
    return pl.pallas_call(
        balance_kernel,
        out_shape=(
            jax.ShapeDtypeStruct((N_ROWS, WIDTH), bf16),
            jax.ShapeDtypeStruct((NZ, WIDTH, QCOLS), bf16),
            jax.ShapeDtypeStruct((HALVES, 8, 128), f32),
            jax.ShapeDtypeStruct((HALVES, 8, 128), f32),
        ),
        in_specs=[hbm, hbm],
        out_specs=(anywhere, anywhere, vmem, vmem),
        scratch_shapes=[
            pltpu.VMEM((FROWS, WIDTH), f32),
            pltpu.VMEM((WIDTH, QCOLS), bf16),
            pltpu.VMEM((N_ROWS, WIDTH), bf16),
            pltpu.VMEM((WIDTH, N_ROWS), bf16),
            pltpu.VMEM((NZ, WIDTH, QCOLS), bf16),
            pltpu.VMEM((NZ, QCOLS, WIDTH), bf16),
            pltpu.VMEM((NZ, N_ROWS, QCOLS), bf16),
            pltpu.VMEM((NZ, QCOLS, N_ROWS), bf16),
            pltpu.VMEM((NZ, QCOLS, N_ROWS), bf16),
            pltpu.VMEM((NZ, 8, QCOLS), f32),
            pltpu.VMEM((ITERS, HALVES, 8, 128), f32),
            pltpu.VMEM((ITERS, HALVES, NZ, 8, 128), f32),
            pltpu.VMEM((ITERS, HALVES, 8, 128), f32),
            pltpu.VMEM((ITERS, HALVES, NP - 1, 8, 128), f32),
            dma((2,)), dma((4,)), dma((4,)), dma((4,)), dma((4,)), dma((4,)), dma((4,)),
            dma((15,)), dma((15,)), dma((16,)), dma((16,)),
            dma((ITERS, HALVES)), dma((ITERS, HALVES)), dma((ITERS, HALVES)), dma((ITERS, HALVES)),
            dma((2,)),
        ],
        compiler_params=pltpu.CompilerParams(
            collective_id=0, has_side_effects=True, vmem_limit_bytes=44 * 2**20
        ),
        cost_estimate=pl.CostEstimate(
            flops=6 * N_ROWS * N_COLS * WIDTH, bytes_accessed=4 * 2**20, transcendentals=3 * N_ROWS * N_COLS
        ),
        name="balance",
    )(features, prototypes)


def write_kernel(f, p, r, c, out, buf, rc, sem):
    steps = N_ROWS // BLOCK
    turned = [jnp.broadcast_to(r[h, i:i + 1, :], (8, 128)).T[:, 0:1] for h in range(HALVES) for i in range(TILES)]
    rc[...] = jnp.concatenate(turned, axis=0)
    rows = [c[g, i:i + 1, :] * float(ROWS * PROTOS) for g in range(HALVES) for i in range(TILES)]
    scale = [jnp.concatenate(rows[4 * q:4 * q + 4], axis=1) for q in range(NZ)]

    def store(i):
        return pltpu.make_async_copy(
            buf.at[i], out.at[pl.ds(pl.multiple_of(i * BLOCK, BLOCK), BLOCK), :], sem.at[i]
        )

    def visit(i, carry):
        rows = pl.ds(pl.multiple_of(i * BLOCK, BLOCK), BLOCK)
        for q in range(NZ):
            s = jnp.dot(f[rows, :], p[q], preferred_element_type=jnp.float32)
            buf[i, :, q * QCOLS:(q + 1) * QCOLS] = jnp.exp2(s * EXP2_SCALE) * rc[rows, :] * scale[q]
        store(i).start()
        return carry

    lax.fori_loop(0, steps, visit, 0)
    for i in range(steps):
        store(i).wait()


def write(f, p, r, c):
    vmem = pl.BlockSpec(memory_space=pltpu.VMEM)
    return pl.pallas_call(
        write_kernel,
        out_shape=jax.ShapeDtypeStruct((N_ROWS, N_COLS), jnp.float32),
        in_specs=[vmem] * 4,
        out_specs=pl.BlockSpec(memory_space=pl.ANY),
        scratch_shapes=[
            pltpu.VMEM((N_ROWS // BLOCK, BLOCK, N_COLS), jnp.float32),
            pltpu.VMEM((N_ROWS, 1), jnp.float32),
            pltpu.SemaphoreType.DMA((N_ROWS // BLOCK,)),
        ],
        compiler_params=pltpu.CompilerParams(vmem_limit_bytes=40 * 2**20),
        cost_estimate=pl.CostEstimate(
            flops=2 * N_ROWS * N_COLS * WIDTH, bytes_accessed=18 * 2**20, transcendentals=N_ROWS * N_COLS
        ),
        name="write",
    )(f, p, r, c)


def body(features, prototypes):
    return write(*balance(features, prototypes))


def solution(mesh):
    in_specs = (P(("batch", "proto"), None), P(None, ("proto", "batch")))
    out_specs = P("batch", "proto")
    return jax.shard_map(body, mesh=mesh, in_specs=in_specs, out_specs=out_specs, check_vma=False)
```

```python
import functools

import jax
import jax.numpy as jnp
from jax import lax
from jax.experimental import pallas as pl
from jax.experimental.pallas import tpu as pltpu
from jax.sharding import PartitionSpec as P

ITERS = 3
PROTOS = 65536
ROWS = 8192
eps = 1e-06
sharpening_divisor = 0.07
LOG2E = 1.4426950408889634
EXP2_SCALE = LOG2E / sharpening_divisor

NZ = 4
NP = 32
N_ROWS = ROWS // NZ
N_COLS = PROTOS // NP
WIDTH = 256
QCOLS = N_COLS // NZ
FROWS = N_ROWS // NP
BLOCK = 256
HALVES = 2
HALF = N_ROWS // HALVES
TILES = HALF // 128
PCHUNK = WIDTH // 4
SLAB = N_ROWS // 4

MESH = pl.DeviceIdType.MESH


def hops(d):
    return sum(min(v, 4 - v) for v in d[:2])


CHIPS = sorted(((dx, dy) for dx in range(4) for dy in range(4) if dx or dy), key=hops, reverse=True)
PEERS = sorted(
    ((dx, dy, dc) for dx in range(4) for dy in range(4) for dc in range(2) if dx or dy or dc),
    key=hops, reverse=True,
)


def operand(dense):
    high = dense.astype(jnp.bfloat16).astype(jnp.float32)
    low = dense - high
    tiles = [
        jnp.concatenate(
            [jnp.broadcast_to(high[i:i + 1], (8, 128)), jnp.broadcast_to(low[i:i + 1], (8, 128))], axis=0
        ).astype(jnp.bfloat16)
        for i in range(dense.shape[0])
    ]
    return jnp.concatenate(tiles, axis=1)


def matvec(parts, matrix):
    return jnp.dot(parts, matrix, preferred_element_type=jnp.float32)


def dense_rows(wide):
    row = lax.broadcasted_iota(jnp.int32, (8, 128), 0)
    out = wide[:, 0:128]
    for i in range(1, wide.shape[1] // 128):
        out = jnp.where(row == i, wide[:, i * 128:(i + 1) * 128], out)
    return out


def join(product):
    return dense_rows(product[0:8] + product[8:16])


def balance_kernel(
    feat_hbm, proto_hbm, f_out, p_out, r_out, c_out,
    feat, proto, fb, ft, pb, pt, e, et, el, col, zs, zr, ps, pr, qs, qr,
    s_in, s_right, s_left, s_fwd, r_left, r_right, r_far,
    s_feat, r_feat, s_sib, r_sib, s_z, r_z, s_p, r_p, s_q, r_q, s_out,
):
    z = lax.axis_index("batch")
    p = lax.axis_index("proto")
    x, y, core = p // 8, (p // 2) % 4, p % 2
    at_x = [((x + d) % 4) * 8 for d in range(4)]
    at_y = [((y + d) % 4) * 2 for d in range(4)]
    at_core = [core, 1 - core]
    at_z = [(z + d) % 4 for d in range(4)]
    right, far, left = at_z[1], at_z[2], at_z[3]

    def plane(dx, dy, dc):
        return at_x[dx % 4] + at_y[dy % 4] + at_core[dc]

    proto_in = pltpu.make_async_copy(proto_hbm, proto, s_in.at[0])
    feat_in = pltpu.make_async_copy(feat_hbm, feat, s_in.at[1])
    proto_in.start()
    feat_in.start()

    barrier = pltpu.get_barrier_semaphore()
    for d in PEERS:
        pl.semaphore_signal(barrier, inc=1, device_id=(z, plane(*d)), device_id_type=MESH)
    for dz in range(1, NZ):
        pl.semaphore_signal(barrier, inc=1, device_id=(at_z[dz], p), device_id_type=MESH)

    def rows_of(owner):
        return pl.ds(pl.multiple_of(owner * FROWS, FROWS), FROWS)

    proto_in.wait()
    raw = proto[...].astype(jnp.float32)
    pb[z] = (raw * lax.rsqrt(jnp.sum(raw * raw, axis=0, keepdims=True) + eps)).astype(jnp.bfloat16)
    feat_in.wait()
    raw = feat[...]
    fb[rows_of(p), :] = (
        raw * lax.rsqrt(jnp.sum(raw * raw, axis=1, keepdims=True) + eps)
    ).astype(jnp.bfloat16)
    col[...] = jnp.zeros_like(col)

    pl.semaphore_wait(barrier, NP - 1 + NZ - 1)

    def send(src, dst, send_sem, recv_sem, target):
        pltpu.make_async_remote_copy(
            src_ref=src, dst_ref=dst, send_sem=send_sem, recv_sem=recv_sem,
            device_id=target, device_id_type=MESH,
        ).start()

    def arrived(ref, sem):
        pltpu.make_async_remote_copy(
            src_ref=ref, dst_ref=ref, send_sem=sem, recv_sem=sem,
            device_id=(right, p), device_id_type=MESH,
        ).wait_recv()

    def sent(ref, sem):
        pltpu.make_async_remote_copy(
            src_ref=ref, dst_ref=ref, send_sem=sem, recv_sem=sem,
            device_id=(right, p), device_id_type=MESH,
        ).wait_send()

    def chunk(owner, k):
        return pb.at[owner, pl.ds(k * PCHUNK, PCHUNK), :]

    for k in range(4):
        kr, kl = k, (k + 2) % 4
        send(chunk(z, kr), chunk(z, kr), s_right.at[kr], r_left.at[kr], (right, p))
        send(chunk(z, kl), chunk(z, kl), s_left.at[kl], r_right.at[kl], (left, p))

    sibling = plane(0, 0, 1)
    mine = fb.at[rows_of(p), :]
    for n, (dx, dy) in enumerate(CHIPS):
        send(mine, mine, s_feat.at[n], r_feat.at[n], (z, plane(dx, dy, 0)))
    send(mine, mine, s_sib.at[15], r_sib.at[15], (z, sibling))

    def pass_features(slab):
        for n, (dx, dy) in enumerate(CHIPS):
            if dx == slab:
                block = fb.at[rows_of(plane(4 - dx, 4 - dy, 0)), :]
                arrived(block, r_feat.at[n])
                send(block, block, s_sib.at[n], r_sib.at[n], (z, sibling))

    def pass_proto(k):
        arrived(chunk(left, k), r_left.at[k])
        send(chunk(left, k), chunk(left, k), s_fwd.at[k], r_far.at[k], (right, p))
        arrived(chunk(right, k + 2), r_right.at[k + 2])
        send(chunk(right, k + 2), chunk(right, k + 2), s_fwd.at[k + 2], r_far.at[k + 2], (left, p))

    def wait_slab(slab):
        for n, (dx, dy) in enumerate(CHIPS):
            if dx == slab:
                arrived(fb.at[rows_of(plane(4 - dx, 4 - dy, 1)), :], r_sib.at[n])
        if slab == 0:
            arrived(fb.at[rows_of(sibling), :], r_sib.at[15])

    def send_columns(it, q):
        for dz in (2, 1, 3):
            send(zs.at[it, q], zr.at[it, q, dz], s_z.at[it, q], r_z.at[it, q], (at_z[dz], p))

    def score_rows(q, start, count):
        rows = pl.ds(pl.multiple_of(start, count), count)
        s = jnp.dot(fb[rows, :], pb[q], preferred_element_type=jnp.float32)
        t = jnp.exp2(s * EXP2_SCALE)
        e[q, rows, :] = t.astype(jnp.bfloat16)
        return jnp.sum(t.reshape(count // 8, 8, QCOLS), axis=0)

    def score_slab(slab):
        col[...] += score_rows(z, at_x[(4 - slab) % 4] * (SLAB // 8), SLAB)

    def score_block(q):
        finish_block(q, score_rows(q, 0, N_ROWS))

    def finish_block(q, total):
        total = jnp.sum(total, axis=0, keepdims=True)
        zs[0, q] = dense_rows(jnp.broadcast_to(total, (8, QCOLS)))
        send_columns(0, q)

    def turn_features():
        ft[...] = fb[...].T

    def score_turned(q, low):
        if not low:
            pt[q] = pb[q].T

        s = jnp.dot(pt[q], ft[...], preferred_element_type=jnp.float32)
        t = jnp.exp2(s * EXP2_SCALE)
        high = t.astype(jnp.bfloat16)
        if low:
            el[q] = (t - high.astype(jnp.float32)).astype(jnp.bfloat16)
        else:
            et[q] = high

    pass_features(0)
    pass_proto(0)
    pass_features(1)
    pass_proto(1)
    pass_features(3)
    wait_slab(0)
    score_slab(0)
    wait_slab(1)
    score_slab(1)
    pass_features(2)
    wait_slab(3)
    score_slab(3)
    wait_slab(2)
    score_slab(2)
    finish_block(z, col[...])
    for k in (2, 3):
        arrived(chunk(left, k), r_left.at[k])
    score_block(left)
    for k in (0, 1):
        arrived(chunk(right, k), r_right.at[k])
    score_block(right)
    for k in range(4):
        arrived(chunk(far, k), r_far.at[k])
    score_block(far)

    f_copy = pltpu.make_async_copy(fb, f_out, s_out.at[0])
    p_copy = pltpu.make_async_copy(pb, p_out, s_out.at[1])
    f_copy.start()
    p_copy.start()
    turn_features()
    for q in (z, left, right, far):
        score_turned(q, False)

    for it in range(ITERS):
        last = it == ITERS - 1
        if it > 0:
            arrived(qr.at[it - 1], r_q.at[it - 1])
            row_sum = qs[it - 1].astype(jnp.float32) + jnp.sum(qr[it - 1].astype(jnp.float32), axis=0)
            parts = operand(1.0 / (ROWS * row_sum))
            for q in range(NZ):
                zs[it, q] = join(matvec(parts, e[q]))
                send_columns(it, q)
        totals = [jnp.zeros((16, HALF), jnp.float32)] * HALVES
        for q in range(NZ):
            arrived(zr.at[it, q, pl.ds(1, NZ - 1)], r_z.at[it, q])
            col_scale = 1.0 / (PROTOS * (zs[it, q] + jnp.sum(zr[it, q, 1:NZ], axis=0)))
            if last:
                c_out[q] = col_scale
            parts = operand(col_scale[0:QCOLS // 128])
            for h in range(HALVES):
                rows = slice(h * HALF, (h + 1) * HALF)
                totals[h] = totals[h] + matvec(parts, et[q, :, rows])
                if last:
                    totals[h] = totals[h] + matvec(parts, el[q, :, rows])
                if last and q == NZ - 1:
                    ps[h] = join(totals[h])
                    for j, d in enumerate(PEERS):
                        send(ps.at[h], pr.at[h, j], s_p.at[h], r_p.at[h], (z, plane(*d)))
        if not last:
            qs[it] = jnp.concatenate([join(t) for t in totals], axis=0).astype(jnp.bfloat16)
            for j, d in enumerate(PEERS):
                send(qs.at[it], qr.at[it, j], s_q.at[it], r_q.at[it], (z, plane(*d)))
        if it == 0:
            for q in range(NZ):
                score_turned(q, True)

    for h in range(HALVES):
        arrived(pr.at[h], r_p.at[h])
        r_out[h] = 1.0 / (ROWS * (ps[h] + jnp.sum(pr[h], axis=0)))

    for k in range(4):
        sent(chunk(z, k), s_right.at[k])
        sent(chunk(z, k), s_left.at[k])
        sent(chunk(z, k), s_fwd.at[k])
    for n in range(15):
        sent(mine, s_feat.at[n])
        sent(mine, s_sib.at[n])
    sent(mine, s_sib.at[15])
    for it in range(ITERS):
        for q in range(NZ):
            sent(zr.at[it, q, pl.ds(1, NZ - 1)], s_z.at[it, q])
    for it in range(ITERS - 1):
        sent(qr.at[it], s_q.at[it])
    for h in range(HALVES):
        sent(pr.at[h], s_p.at[h])
    f_copy.wait()
    p_copy.wait()


def balance(features, prototypes):
    f32, bf16 = jnp.float32, jnp.bfloat16
    vmem = pl.BlockSpec(memory_space=pltpu.VMEM)
    anywhere = pl.BlockSpec(memory_space=pl.ANY)
    hbm = pl.BlockSpec(memory_space=pltpu.HBM)
    dma = pltpu.SemaphoreType.DMA
    return pl.pallas_call(
        balance_kernel,
        out_shape=(
            jax.ShapeDtypeStruct((N_ROWS, WIDTH), bf16),
            jax.ShapeDtypeStruct((NZ, WIDTH, QCOLS), bf16),
            jax.ShapeDtypeStruct((HALVES, 8, 128), f32),
            jax.ShapeDtypeStruct((NZ, 8, 128), f32),
        ),
        in_specs=[hbm, hbm],
        out_specs=(anywhere, anywhere, vmem, vmem),
        scratch_shapes=[
            pltpu.VMEM((FROWS, WIDTH), f32),
            pltpu.VMEM((WIDTH, QCOLS), bf16),
            pltpu.VMEM((N_ROWS, WIDTH), bf16),
            pltpu.VMEM((WIDTH, N_ROWS), bf16),
            pltpu.VMEM((NZ, WIDTH, QCOLS), bf16),
            pltpu.VMEM((NZ, QCOLS, WIDTH), bf16),
            pltpu.VMEM((NZ, N_ROWS, QCOLS), bf16),
            pltpu.VMEM((NZ, QCOLS, N_ROWS), bf16),
            pltpu.VMEM((NZ, QCOLS, N_ROWS), bf16),
            pltpu.VMEM((8, QCOLS), f32),
            pltpu.VMEM((ITERS, NZ, 8, 128), f32),
            pltpu.VMEM((ITERS, NZ, NZ, 8, 128), f32),
            pltpu.VMEM((HALVES, 8, 128), f32),
            pltpu.VMEM((HALVES, NP - 1, 8, 128), f32),
            pltpu.VMEM((ITERS - 1, 16, 128), bf16),
            pltpu.VMEM((ITERS - 1, NP - 1, 16, 128), bf16),
            dma((2,)), dma((4,)), dma((4,)), dma((4,)), dma((4,)), dma((4,)), dma((4,)),
            dma((15,)), dma((15,)), dma((16,)), dma((16,)),
            dma((ITERS, NZ)), dma((ITERS, NZ)), dma((HALVES,)), dma((HALVES,)), dma((ITERS - 1,)), dma((ITERS - 1,)),
            dma((2,)),
        ],
        compiler_params=pltpu.CompilerParams(
            collective_id=0, has_side_effects=True, vmem_limit_bytes=44 * 2**20
        ),
        cost_estimate=pl.CostEstimate(
            flops=6 * N_ROWS * N_COLS * WIDTH, bytes_accessed=4 * 2**20, transcendentals=3 * N_ROWS * N_COLS
        ),
        name="balance",
    )(*(pltpu.with_memory_space_constraint(a, pltpu.HBM) for a in (features, prototypes)))


def write_kernel(f, p, r, c, out, buf, rc, sem):
    steps = N_ROWS // BLOCK
    turned = [jnp.broadcast_to(r[h, i:i + 1, :], (8, 128)).T[:, 0:1] for h in range(HALVES) for i in range(TILES)]
    rc[...] = jnp.concatenate(turned, axis=0)
    scale = [
        jnp.concatenate([c[q, i:i + 1, :] * float(ROWS * PROTOS) for i in range(QCOLS // 128)], axis=1)
        for q in range(NZ)
    ]

    def store(i):
        return pltpu.make_async_copy(
            buf.at[i], out.at[pl.ds(pl.multiple_of(i * BLOCK, BLOCK), BLOCK), :], sem.at[i]
        )

    def visit(i, carry):
        rows = pl.ds(pl.multiple_of(i * BLOCK, BLOCK), BLOCK)
        for q in range(NZ):
            s = jnp.dot(f[rows, :], p[q], preferred_element_type=jnp.float32)
            buf[i, :, q * QCOLS:(q + 1) * QCOLS] = jnp.exp2(s * EXP2_SCALE) * rc[rows, :] * scale[q]
        store(i).start()
        return carry

    lax.fori_loop(0, steps, visit, 0)
    for i in range(steps):
        store(i).wait()


def write(f, p, r, c):
    vmem = pl.BlockSpec(memory_space=pltpu.VMEM)
    return pl.pallas_call(
        write_kernel,
        out_shape=jax.ShapeDtypeStruct((N_ROWS, N_COLS), jnp.float32),
        in_specs=[vmem] * 4,
        out_specs=pl.BlockSpec(memory_space=pl.ANY),
        scratch_shapes=[
            pltpu.VMEM((N_ROWS // BLOCK, BLOCK, N_COLS), jnp.float32),
            pltpu.VMEM((N_ROWS, 1), jnp.float32),
            pltpu.SemaphoreType.DMA((N_ROWS // BLOCK,)),
        ],
        compiler_params=pltpu.CompilerParams(vmem_limit_bytes=40 * 2**20),
        cost_estimate=pl.CostEstimate(
            flops=2 * N_ROWS * N_COLS * WIDTH, bytes_accessed=18 * 2**20, transcendentals=N_ROWS * N_COLS
        ),
        name="write",
    )(f, p, r, c)


def body(features, prototypes):
    return write(*balance(features, prototypes))


def solution(mesh):
    in_specs = (P(("batch", "proto"), None), P(None, ("proto", "batch")))
    out_specs = P("batch", "proto")
    return jax.shard_map(body, mesh=mesh, in_specs=in_specs, out_specs=out_specs, check_vma=False)
```

```python
import functools

import jax
import jax.numpy as jnp
from jax import lax
from jax.experimental import pallas as pl
from jax.experimental.pallas import tpu as pltpu
from jax.sharding import PartitionSpec as P

ITERS = 3
PROTOS = 65536
ROWS = 8192
eps = 1e-06
sharpening_divisor = 0.07
LOG2E = 1.4426950408889634
EXP2_SCALE = LOG2E / sharpening_divisor

NZ = 4
NP = 32
N_ROWS = ROWS // NZ
N_COLS = PROTOS // NP
WIDTH = 256
QCOLS = N_COLS // NZ
FROWS = N_ROWS // NP
BLOCK = 256
HALVES = 2
HALF = N_ROWS // HALVES
TILES = HALF // 128
PCHUNK = WIDTH // 4
SLAB = N_ROWS // 4

MESH = pl.DeviceIdType.MESH


def hops(d):
    return sum(min(v, 4 - v) for v in d[:2])


CHIPS = sorted(((dx, dy) for dx in range(4) for dy in range(4) if dx or dy), key=hops, reverse=True)
PEERS = sorted(
    ((dx, dy, dc) for dx in range(4) for dy in range(4) for dc in range(2) if dx or dy or dc),
    key=hops, reverse=True,
)
NEAR = [(2, 0, 0), (0, 2, 0), (1, 0, 0), (3, 0, 0), (0, 1, 0), (0, 3, 0), (0, 0, 1)]


def operand(dense):
    high = dense.astype(jnp.bfloat16).astype(jnp.float32)
    low = dense - high
    tiles = [
        jnp.concatenate(
            [jnp.broadcast_to(high[i:i + 1], (8, 128)), jnp.broadcast_to(low[i:i + 1], (8, 128))], axis=0
        ).astype(jnp.bfloat16)
        for i in range(dense.shape[0])
    ]
    return jnp.concatenate(tiles, axis=1)


def matvec(parts, matrix):
    return jnp.dot(parts, matrix, preferred_element_type=jnp.float32)


def dense_rows(wide):
    row = lax.broadcasted_iota(jnp.int32, (8, 128), 0)
    out = wide[:, 0:128]
    for i in range(1, wide.shape[1] // 128):
        out = jnp.where(row == i, wide[:, i * 128:(i + 1) * 128], out)
    return out


def join(product):
    return dense_rows(product[0:8] + product[8:16])


def balance_kernel(
    feat_hbm, proto_hbm, f_out, p_out, r_out, c_out,
    feat, proto, fb, ft, pb, pt, e, et, el, col, zs, zr, ps, pr, qs, qr,
    s_in, s_right, s_left, s_fwd, r_left, r_right, r_far,
    s_feat, r_feat, s_sib, r_sib, s_z, r_z, s_p, r_p, s_q, r_q, s_out, greeted,
):
    z = lax.axis_index("batch")
    p = lax.axis_index("proto")
    x, y, core = p // 8, (p // 2) % 4, p % 2
    at_x = [((x + d) % 4) * 8 for d in range(4)]
    at_y = [((y + d) % 4) * 2 for d in range(4)]
    at_core = [core, 1 - core]
    at_z = [(z + d) % 4 for d in range(4)]
    right, far, left = at_z[1], at_z[2], at_z[3]

    def plane(dx, dy, dc):
        return at_x[dx % 4] + at_y[dy % 4] + at_core[dc]

    barrier = pltpu.get_barrier_semaphore()
    for dz in (2, 1, 3):
        pl.semaphore_signal(barrier, inc=1, device_id=(at_z[dz], p), device_id_type=MESH)
    for d in NEAR:
        pl.semaphore_signal(barrier, inc=1, device_id=(z, plane(*d)), device_id_type=MESH)

    proto_in = pltpu.make_async_copy(proto_hbm, proto, s_in.at[0])
    feat_in = pltpu.make_async_copy(feat_hbm, feat, s_in.at[1])
    proto_in.start()
    feat_in.start()

    def rows_of(owner):
        return pl.ds(pl.multiple_of(owner * FROWS, FROWS), FROWS)

    proto_in.wait()
    raw = proto[...].astype(jnp.float32)
    pb[z] = (raw * lax.rsqrt(jnp.sum(raw * raw, axis=0, keepdims=True) + eps)).astype(jnp.bfloat16)
    feat_in.wait()
    raw = feat[...]
    fb[rows_of(p), :] = (
        raw * lax.rsqrt(jnp.sum(raw * raw, axis=1, keepdims=True) + eps)
    ).astype(jnp.bfloat16)

    pl.semaphore_wait(barrier, NZ - 1 + len(NEAR))

    def send(src, dst, send_sem, recv_sem, target):
        pltpu.make_async_remote_copy(
            src_ref=src, dst_ref=dst, send_sem=send_sem, recv_sem=recv_sem,
            device_id=target, device_id_type=MESH,
        ).start()

    def arrived(ref, sem):
        pltpu.make_async_remote_copy(
            src_ref=ref, dst_ref=ref, send_sem=sem, recv_sem=sem,
            device_id=(right, p), device_id_type=MESH,
        ).wait_recv()

    def sent(ref, sem):
        pltpu.make_async_remote_copy(
            src_ref=ref, dst_ref=ref, send_sem=sem, recv_sem=sem,
            device_id=(right, p), device_id_type=MESH,
        ).wait_send()

    def chunk(owner, k):
        return pb.at[owner, pl.ds(k * PCHUNK, PCHUNK), :]

    for k in range(4):
        kr, kl = k, (k + 2) % 4
        send(chunk(z, kr), chunk(z, kr), s_right.at[kr], r_left.at[kr], (right, p))
        send(chunk(z, kl), chunk(z, kl), s_left.at[kl], r_right.at[kl], (left, p))

    sibling = plane(0, 0, 1)
    mine = fb.at[rows_of(p), :]
    def send_features(slabs):
        for n, (dx, dy) in enumerate(CHIPS):
            if dx in slabs:
                send(mine, mine, s_feat.at[n], r_feat.at[n], (z, plane(dx, dy, 0)))

    for dx in (2, 1, 3):
        pl.semaphore_signal(greeted, inc=1, device_id=(z, plane(dx, 0, 0)), device_id_type=MESH)
    send_features((0,))
    send(mine, mine, s_sib.at[15], r_sib.at[15], (z, sibling))
    pl.semaphore_wait(greeted, 3)
    send_features((1, 2, 3))

    def pass_features(slab):
        for n, (dx, dy) in enumerate(CHIPS):
            if dx == slab:
                block = fb.at[rows_of(plane(4 - dx, 4 - dy, 0)), :]
                arrived(block, r_feat.at[n])
                send(block, block, s_sib.at[n], r_sib.at[n], (z, sibling))

    def pass_proto(k):
        arrived(chunk(left, k), r_left.at[k])
        send(chunk(left, k), chunk(left, k), s_fwd.at[k], r_far.at[k], (right, p))
        arrived(chunk(right, k + 2), r_right.at[k + 2])
        send(chunk(right, k + 2), chunk(right, k + 2), s_fwd.at[k + 2], r_far.at[k + 2], (left, p))

    def wait_slab(slab):
        for n, (dx, dy) in enumerate(CHIPS):
            if dx == slab:
                arrived(fb.at[rows_of(plane(4 - dx, 4 - dy, 1)), :], r_sib.at[n])
        if slab == 0:
            arrived(fb.at[rows_of(sibling), :], r_sib.at[15])

    def send_columns(it, q):
        for dz in (2, 1, 3):
            send(zs.at[it, q], zr.at[it, q, dz], s_z.at[it, q], r_z.at[it, q], (at_z[dz], p))

    def score_rows(q, start, count):
        rows = pl.ds(pl.multiple_of(start, count), count)
        s = jnp.dot(fb[rows, :], pb[q], preferred_element_type=jnp.float32)
        t = jnp.exp2(s * EXP2_SCALE)
        e[q, rows, :] = t.astype(jnp.bfloat16)
        return jnp.sum(t.reshape(count // 8, 8, QCOLS), axis=0)

    def score_slab(q, slab):
        return score_rows(q, at_x[(4 - slab) % 4] * (SLAB // 8), SLAB)

    def finish_block(q, total):
        total = jnp.sum(total, axis=0, keepdims=True)
        zs[0, q] = dense_rows(jnp.broadcast_to(total, (8, QCOLS)))
        send_columns(0, q)

    def turn_features():
        ft[...] = fb[...].T

    def score_turned(q, low):
        if not low:
            pt[q] = pb[q].T

        s = jnp.dot(pt[q], ft[...], preferred_element_type=jnp.float32)
        t = jnp.exp2(s * EXP2_SCALE)
        high = t.astype(jnp.bfloat16)
        if low:
            el[q] = (t - high.astype(jnp.float32)).astype(jnp.bfloat16)
        else:
            et[q] = high

    pass_features(0)
    pass_proto(0)
    pass_features(1)
    pass_proto(1)
    pass_features(3)
    wait_slab(0)
    col[0] = score_slab(z, 0)
    wait_slab(1)
    col[0] += score_slab(z, 1)
    pass_features(2)
    wait_slab(3)
    col[0] += score_slab(z, 3)
    for k in (2, 3):
        arrived(chunk(left, k), r_left.at[k])
    for k in (0, 1):
        arrived(chunk(right, k), r_right.at[k])
    for i, q in ((1, left), (2, right)):
        col[i] = score_slab(q, 0) + score_slab(q, 1) + score_slab(q, 3)
    wait_slab(2)
    for i, q in enumerate((z, left, right)):
        finish_block(q, col[i] + score_slab(q, 2))
    for k in range(4):
        arrived(chunk(far, k), r_far.at[k])
    finish_block(far, score_rows(far, 0, N_ROWS))

    f_copy = pltpu.make_async_copy(fb, f_out, s_out.at[0])
    p_copy = pltpu.make_async_copy(pb, p_out, s_out.at[1])
    f_copy.start()
    p_copy.start()
    turn_features()
    for q in (z, left, right, far):
        score_turned(q, False)

    for it in range(ITERS):
        last = it == ITERS - 1
        if it > 0:
            arrived(qr.at[it - 1], r_q.at[it - 1])
            row_sum = qs[it - 1].astype(jnp.float32) + jnp.sum(qr[it - 1].astype(jnp.float32), axis=0)
            parts = operand(1.0 / (ROWS * row_sum))
            for q in range(NZ):
                zs[it, q] = join(matvec(parts, e[q]))
                send_columns(it, q)
        totals = [jnp.zeros((16, HALF), jnp.float32)] * HALVES
        for q in range(NZ):
            arrived(zr.at[it, q, pl.ds(1, NZ - 1)], r_z.at[it, q])
            col_scale = 1.0 / (PROTOS * (zs[it, q] + jnp.sum(zr[it, q, 1:NZ], axis=0)))
            if last:
                c_out[q] = col_scale
            parts = operand(col_scale[0:QCOLS // 128])
            for h in range(HALVES):
                rows = slice(h * HALF, (h + 1) * HALF)
                totals[h] = totals[h] + matvec(parts, et[q, :, rows])
                if last:
                    totals[h] = totals[h] + matvec(parts, el[q, :, rows])
                if last and q == NZ - 1:
                    ps[h] = join(totals[h])
                    for j, d in enumerate(PEERS):
                        send(ps.at[h], pr.at[h, j], s_p.at[h], r_p.at[h], (z, plane(*d)))
        if not last:
            qs[it] = jnp.concatenate([join(t) for t in totals], axis=0).astype(jnp.bfloat16)
            for j, d in enumerate(PEERS):
                send(qs.at[it], qr.at[it, j], s_q.at[it], r_q.at[it], (z, plane(*d)))
        if it == 0:
            for q in range(NZ):
                score_turned(q, True)

    for h in range(HALVES):
        arrived(pr.at[h], r_p.at[h])
        r_out[h] = 1.0 / (ROWS * (ps[h] + jnp.sum(pr[h], axis=0)))

    for k in range(4):
        sent(chunk(z, k), s_right.at[k])
        sent(chunk(z, k), s_left.at[k])
        sent(chunk(z, k), s_fwd.at[k])
    for n in range(15):
        sent(mine, s_feat.at[n])
        sent(mine, s_sib.at[n])
    sent(mine, s_sib.at[15])
    for it in range(ITERS):
        for q in range(NZ):
            sent(zr.at[it, q, pl.ds(1, NZ - 1)], s_z.at[it, q])
    for it in range(ITERS - 1):
        sent(qr.at[it], s_q.at[it])
    for h in range(HALVES):
        sent(pr.at[h], s_p.at[h])
    f_copy.wait()
    p_copy.wait()


def balance(features, prototypes):
    f32, bf16 = jnp.float32, jnp.bfloat16
    vmem = pl.BlockSpec(memory_space=pltpu.VMEM)
    anywhere = pl.BlockSpec(memory_space=pl.ANY)
    hbm = pl.BlockSpec(memory_space=pltpu.HBM)
    dma = pltpu.SemaphoreType.DMA
    return pl.pallas_call(
        balance_kernel,
        out_shape=(
            jax.ShapeDtypeStruct((N_ROWS, WIDTH), bf16),
            jax.ShapeDtypeStruct((NZ, WIDTH, QCOLS), bf16),
            jax.ShapeDtypeStruct((HALVES, 8, 128), f32),
            jax.ShapeDtypeStruct((NZ, 8, 128), f32),
        ),
        in_specs=[hbm, hbm],
        out_specs=(anywhere, anywhere, vmem, vmem),
        scratch_shapes=[
            pltpu.VMEM((FROWS, WIDTH), f32),
            pltpu.VMEM((WIDTH, QCOLS), bf16),
            pltpu.VMEM((N_ROWS, WIDTH), bf16),
            pltpu.VMEM((WIDTH, N_ROWS), bf16),
            pltpu.VMEM((NZ, WIDTH, QCOLS), bf16),
            pltpu.VMEM((NZ, QCOLS, WIDTH), bf16),
            pltpu.VMEM((NZ, N_ROWS, QCOLS), bf16),
            pltpu.VMEM((NZ, QCOLS, N_ROWS), bf16),
            pltpu.VMEM((NZ, QCOLS, N_ROWS), bf16),
            pltpu.VMEM((3, 8, QCOLS), f32),
            pltpu.VMEM((ITERS, NZ, 8, 128), f32),
            pltpu.VMEM((ITERS, NZ, NZ, 8, 128), f32),
            pltpu.VMEM((HALVES, 8, 128), f32),
            pltpu.VMEM((HALVES, NP - 1, 8, 128), f32),
            pltpu.VMEM((ITERS - 1, 16, 128), bf16),
            pltpu.VMEM((ITERS - 1, NP - 1, 16, 128), bf16),
            dma((2,)), dma((4,)), dma((4,)), dma((4,)), dma((4,)), dma((4,)), dma((4,)),
            dma((15,)), dma((15,)), dma((16,)), dma((16,)),
            dma((ITERS, NZ)), dma((ITERS, NZ)), dma((HALVES,)), dma((HALVES,)), dma((ITERS - 1,)), dma((ITERS - 1,)),
            dma((2,)), pltpu.SemaphoreType.REGULAR,
        ],
        compiler_params=pltpu.CompilerParams(
            collective_id=0, has_side_effects=True, vmem_limit_bytes=44 * 2**20
        ),
        cost_estimate=pl.CostEstimate(
            flops=6 * N_ROWS * N_COLS * WIDTH, bytes_accessed=4 * 2**20, transcendentals=3 * N_ROWS * N_COLS
        ),
        name="balance",
    )(*(pltpu.with_memory_space_constraint(a, pltpu.HBM) for a in (features, prototypes)))


def write_kernel(f, p, r, c, out, buf, rc, sem):
    steps = N_ROWS // BLOCK
    turned = [jnp.broadcast_to(r[h, i:i + 1, :], (8, 128)).T[:, 0:1] for h in range(HALVES) for i in range(TILES)]
    rc[...] = jnp.concatenate(turned, axis=0)
    scale = [
        jnp.concatenate([c[q, i:i + 1, :] * float(ROWS * PROTOS) for i in range(QCOLS // 128)], axis=1)
        for q in range(NZ)
    ]

    def store(i):
        return pltpu.make_async_copy(
            buf.at[i], out.at[pl.ds(pl.multiple_of(i * BLOCK, BLOCK), BLOCK), :], sem.at[i]
        )

    def visit(i, carry):
        rows = pl.ds(pl.multiple_of(i * BLOCK, BLOCK), BLOCK)
        for q in range(NZ):
            s = jnp.dot(f[rows, :], p[q], preferred_element_type=jnp.float32)
            buf[i, :, q * QCOLS:(q + 1) * QCOLS] = jnp.exp2(s * EXP2_SCALE) * rc[rows, :] * scale[q]
        store(i).start()
        return carry

    lax.fori_loop(0, steps, visit, 0)
    for i in range(steps):
        store(i).wait()


def write(f, p, r, c):
    vmem = pl.BlockSpec(memory_space=pltpu.VMEM)
    return pl.pallas_call(
        write_kernel,
        out_shape=jax.ShapeDtypeStruct((N_ROWS, N_COLS), jnp.float32),
        in_specs=[vmem] * 4,
        out_specs=pl.BlockSpec(memory_space=pl.ANY),
        scratch_shapes=[
            pltpu.VMEM((N_ROWS // BLOCK, BLOCK, N_COLS), jnp.float32),
            pltpu.VMEM((N_ROWS, 1), jnp.float32),
            pltpu.SemaphoreType.DMA((N_ROWS // BLOCK,)),
        ],
        compiler_params=pltpu.CompilerParams(vmem_limit_bytes=40 * 2**20),
        cost_estimate=pl.CostEstimate(
            flops=2 * N_ROWS * N_COLS * WIDTH, bytes_accessed=18 * 2**20, transcendentals=N_ROWS * N_COLS
        ),
        name="write",
    )(f, p, r, c)


def body(features, prototypes):
    return write(*balance(features, prototypes))


def solution(mesh):
    in_specs = (P(("batch", "proto"), None), P(None, ("proto", "batch")))
    out_specs = P("batch", "proto")
    return jax.shard_map(body, mesh=mesh, in_specs=in_specs, out_specs=out_specs, check_vma=False)
```

```python
import functools

import jax
import jax.numpy as jnp
from jax import lax
from jax.experimental import pallas as pl
from jax.experimental.pallas import tpu as pltpu
from jax.sharding import PartitionSpec as P

ITERS = 3
PROTOS = 65536
ROWS = 8192
eps = 1e-06
sharpening_divisor = 0.07
LOG2E = 1.4426950408889634
EXP2_SCALE = LOG2E / sharpening_divisor

NZ = 4
NP = 32
N_ROWS = ROWS // NZ
N_COLS = PROTOS // NP
WIDTH = 256
QCOLS = N_COLS // NZ
FROWS = N_ROWS // NP
BLOCK = 256
HALVES = 2
HALF = N_ROWS // HALVES
TILES = HALF // 128
PCHUNK = WIDTH // 4
SLAB = N_ROWS // 4

MESH = pl.DeviceIdType.MESH


def hops(d):
    return sum(min(v, 4 - v) for v in d[:2])


CHIPS = sorted(((dx, dy) for dx in range(4) for dy in range(4) if dx or dy), key=hops, reverse=True)
PEERS = sorted(
    ((dx, dy, dc) for dx in range(4) for dy in range(4) for dc in range(2) if dx or dy or dc),
    key=hops, reverse=True,
)
NEAR = [(2, 0, 0), (0, 2, 0), (1, 0, 0), (3, 0, 0), (0, 1, 0), (0, 3, 0), (0, 0, 1)]


def operand(dense):
    high = dense.astype(jnp.bfloat16).astype(jnp.float32)
    low = dense - high
    tiles = [
        jnp.concatenate(
            [jnp.broadcast_to(high[i:i + 1], (8, 128)), jnp.broadcast_to(low[i:i + 1], (8, 128))], axis=0
        ).astype(jnp.bfloat16)
        for i in range(dense.shape[0])
    ]
    return jnp.concatenate(tiles, axis=1)


def matvec(parts, matrix):
    return jnp.dot(parts, matrix, preferred_element_type=jnp.float32)


def dense_rows(wide):
    row = lax.broadcasted_iota(jnp.int32, (8, 128), 0)
    out = wide[:, 0:128]
    for i in range(1, wide.shape[1] // 128):
        out = jnp.where(row == i, wide[:, i * 128:(i + 1) * 128], out)
    return out


def join(product):
    return dense_rows(product[0:8] + product[8:16])


def balance_kernel(
    feat_hbm, proto_hbm, f_out, p_out, r_out, c_out,
    feat, proto, fb, ft, pb, pt, e, et, el, col, zs, zr, ps, pr, qs, qr,
    s_in, s_right, s_left, s_fwd, r_left, r_right, r_far,
    s_feat, r_feat, s_sib, r_sib, s_z, r_z, s_p, r_p, s_q, r_q, s_out, greeted,
):
    z = lax.axis_index("batch")
    p = lax.axis_index("proto")
    x, y, core = p // 8, (p // 2) % 4, p % 2
    at_x = [((x + d) % 4) * 8 for d in range(4)]
    at_y = [((y + d) % 4) * 2 for d in range(4)]
    at_core = [core, 1 - core]
    at_z = [(z + d) % 4 for d in range(4)]
    right, far, left = at_z[1], at_z[2], at_z[3]

    def plane(dx, dy, dc):
        return at_x[dx % 4] + at_y[dy % 4] + at_core[dc]

    barrier = pltpu.get_barrier_semaphore()
    for dz in (2, 1, 3):
        pl.semaphore_signal(barrier, inc=1, device_id=(at_z[dz], p), device_id_type=MESH)
    for d in NEAR:
        pl.semaphore_signal(barrier, inc=1, device_id=(z, plane(*d)), device_id_type=MESH)

    proto_in = pltpu.make_async_copy(proto_hbm, proto, s_in.at[0])
    feat_in = pltpu.make_async_copy(feat_hbm, feat, s_in.at[1])
    proto_in.start()
    feat_in.start()

    def rows_of(owner):
        return pl.ds(pl.multiple_of(owner * FROWS, FROWS), FROWS)

    proto_in.wait()
    raw = proto[...].astype(jnp.float32)
    pb[z] = (raw * lax.rsqrt(jnp.sum(raw * raw, axis=0, keepdims=True) + eps)).astype(jnp.bfloat16)
    feat_in.wait()
    raw = feat[...]
    fb[rows_of(p), :] = (
        raw * lax.rsqrt(jnp.sum(raw * raw, axis=1, keepdims=True) + eps)
    ).astype(jnp.bfloat16)

    pl.semaphore_wait(barrier, NZ - 1 + len(NEAR))

    def send(src, dst, send_sem, recv_sem, target):
        pltpu.make_async_remote_copy(
            src_ref=src, dst_ref=dst, send_sem=send_sem, recv_sem=recv_sem,
            device_id=target, device_id_type=MESH,
        ).start()

    def arrived(ref, sem):
        pltpu.make_async_remote_copy(
            src_ref=ref, dst_ref=ref, send_sem=sem, recv_sem=sem,
            device_id=(right, p), device_id_type=MESH,
        ).wait_recv()

    def sent(ref, sem):
        pltpu.make_async_remote_copy(
            src_ref=ref, dst_ref=ref, send_sem=sem, recv_sem=sem,
            device_id=(right, p), device_id_type=MESH,
        ).wait_send()

    def chunk(owner, k):
        return pb.at[owner, pl.ds(k * PCHUNK, PCHUNK), :]

    for k in range(4):
        kr, kl = k, (k + 2) % 4
        send(chunk(z, kr), chunk(z, kr), s_right.at[kr], r_left.at[kr], (right, p))
        send(chunk(z, kl), chunk(z, kl), s_left.at[kl], r_right.at[kl], (left, p))

    sibling = plane(0, 0, 1)
    mine = fb.at[rows_of(p), :]
    def send_features(slabs):
        for n, (dx, dy) in enumerate(CHIPS):
            if dx in slabs:
                send(mine, mine, s_feat.at[n], r_feat.at[n], (z, plane(dx, dy, 0)))

    for dx in (2, 1, 3):
        pl.semaphore_signal(greeted, inc=1, device_id=(z, plane(dx, 0, 0)), device_id_type=MESH)
    send_features((0,))
    send(mine, mine, s_sib.at[15], r_sib.at[15], (z, sibling))
    pl.semaphore_wait(greeted, 3)
    send_features((1, 2, 3))

    def pass_features(slab):
        for n, (dx, dy) in enumerate(CHIPS):
            if dx == slab:
                block = fb.at[rows_of(plane(4 - dx, 4 - dy, 0)), :]
                arrived(block, r_feat.at[n])
                send(block, block, s_sib.at[n], r_sib.at[n], (z, sibling))

    def pass_proto(k):
        arrived(chunk(left, k), r_left.at[k])
        send(chunk(left, k), chunk(left, k), s_fwd.at[k], r_far.at[k], (right, p))
        arrived(chunk(right, k + 2), r_right.at[k + 2])
        send(chunk(right, k + 2), chunk(right, k + 2), s_fwd.at[k + 2], r_far.at[k + 2], (left, p))

    def wait_slab(slab):
        for n, (dx, dy) in enumerate(CHIPS):
            if dx == slab:
                arrived(fb.at[rows_of(plane(4 - dx, 4 - dy, 1)), :], r_sib.at[n])
        if slab == 0:
            arrived(fb.at[rows_of(sibling), :], r_sib.at[15])

    def send_columns(it, q):
        for dz in (2, 1, 3):
            send(zs.at[it, q], zr.at[it, q, dz], s_z.at[it, q], r_z.at[it, q], (at_z[dz], p))

    def score_rows(q, start, count):
        rows = pl.ds(pl.multiple_of(start, count), count)
        s = jnp.dot(fb[rows, :], pb[q], preferred_element_type=jnp.float32)
        t = jnp.exp2(s * EXP2_SCALE)
        e[q, rows, :] = t.astype(jnp.bfloat16)
        return jnp.sum(t.reshape(count // 8, 8, QCOLS), axis=0)

    def score_slab(q, slab):
        return score_rows(q, at_x[(4 - slab) % 4] * (SLAB // 8), SLAB)

    def finish_block(q, total):
        total = jnp.sum(total, axis=0, keepdims=True)
        zs[0, q] = dense_rows(jnp.broadcast_to(total, (8, QCOLS)))
        send_columns(0, q)

    def turn_features():
        ft[...] = fb[...].T

    def score_turned(q, low):
        if not low:
            pt[q] = pb[q].T

        s = jnp.dot(pt[q], ft[...], preferred_element_type=jnp.float32)
        t = jnp.exp2(s * EXP2_SCALE)
        high = t.astype(jnp.bfloat16)
        if low:
            el[q] = (t - high.astype(jnp.float32)).astype(jnp.bfloat16)
        else:
            et[q] = high

    pass_features(0)
    pass_proto(0)
    pass_features(1)
    pass_proto(1)
    pass_features(3)
    wait_slab(0)
    col[0] = score_slab(z, 0)
    wait_slab(1)
    col[0] += score_slab(z, 1)
    pass_features(2)
    wait_slab(3)
    col[0] += score_slab(z, 3)
    for k in (2, 3):
        arrived(chunk(left, k), r_left.at[k])
    for k in (0, 1):
        arrived(chunk(right, k), r_right.at[k])
    for i, q in ((1, left), (2, right)):
        col[i] = score_slab(q, 0) + score_slab(q, 1) + score_slab(q, 3)
    wait_slab(2)
    for i, q in enumerate((z, left, right)):
        finish_block(q, col[i] + score_slab(q, 2))
    for k in range(4):
        arrived(chunk(far, k), r_far.at[k])
    finish_block(far, score_rows(far, 0, N_ROWS))

    f_copy = pltpu.make_async_copy(fb, f_out, s_out.at[0])
    p_copy = pltpu.make_async_copy(pb, p_out, s_out.at[1])
    f_copy.start()
    p_copy.start()
    turn_features()
    for q in (z, left, right, far):
        score_turned(q, False)

    for it in range(ITERS):
        last = it == ITERS - 1
        if it > 0:
            arrived(qr.at[it - 1], r_q.at[it - 1])
            row_sum = qs[it - 1].astype(jnp.float32) + jnp.sum(qr[it - 1].astype(jnp.float32), axis=0)
            parts = operand(1.0 / (ROWS * row_sum))
            for q in range(NZ):
                zs[it, q] = join(matvec(parts, e[q]))
                send_columns(it, q)
        totals = [jnp.zeros((16, HALF), jnp.float32)] * HALVES
        for q in range(NZ):
            arrived(zr.at[it, q, pl.ds(1, NZ - 1)], r_z.at[it, q])
            col_scale = 1.0 / (PROTOS * (zs[it, q] + jnp.sum(zr[it, q, 1:NZ], axis=0)))
            if last:
                c_out[q] = col_scale
            parts = operand(col_scale[0:QCOLS // 128])
            for h in range(HALVES):
                rows = slice(h * HALF, (h + 1) * HALF)
                totals[h] = totals[h] + matvec(parts, et[q, :, rows])
                if last:
                    totals[h] = totals[h] + matvec(parts, el[q, :, rows])
                if last and q == NZ - 1:
                    ps[h * 8:(h + 1) * 8, :] = join(totals[h])
        if last:
            for j, d in enumerate(PEERS):
                send(ps, pr.at[j], s_p, r_p, (z, plane(*d)))
        if not last:
            qs[it] = jnp.concatenate([join(t) for t in totals], axis=0).astype(jnp.bfloat16)
            for j, d in enumerate(PEERS):
                send(qs.at[it], qr.at[it, j], s_q.at[it], r_q.at[it], (z, plane(*d)))
        if it == 0:
            for q in range(NZ):
                score_turned(q, True)

    for k in range(4):
        sent(chunk(z, k), s_right.at[k])
        sent(chunk(z, k), s_left.at[k])
        sent(chunk(z, k), s_fwd.at[k])
    for n in range(15):
        sent(mine, s_feat.at[n])
        sent(mine, s_sib.at[n])
    sent(mine, s_sib.at[15])
    for it in range(ITERS):
        for q in range(NZ):
            sent(zr.at[it, q, pl.ds(1, NZ - 1)], s_z.at[it, q])
    for it in range(ITERS - 1):
        sent(qr.at[it], s_q.at[it])
    f_copy.wait()
    p_copy.wait()

    arrived(pr, r_p)
    scale = 1.0 / (ROWS * (ps[...] + jnp.sum(pr[...], axis=0)))
    for h in range(HALVES):
        r_out[h] = scale[h * 8:(h + 1) * 8]

    sent(pr, s_p)


def balance(features, prototypes):
    f32, bf16 = jnp.float32, jnp.bfloat16
    vmem = pl.BlockSpec(memory_space=pltpu.VMEM)
    anywhere = pl.BlockSpec(memory_space=pl.ANY)
    hbm = pl.BlockSpec(memory_space=pltpu.HBM)
    dma = pltpu.SemaphoreType.DMA
    return pl.pallas_call(
        balance_kernel,
        out_shape=(
            jax.ShapeDtypeStruct((N_ROWS, WIDTH), bf16),
            jax.ShapeDtypeStruct((NZ, WIDTH, QCOLS), bf16),
            jax.ShapeDtypeStruct((HALVES, 8, 128), f32),
            jax.ShapeDtypeStruct((NZ, 8, 128), f32),
        ),
        in_specs=[hbm, hbm],
        out_specs=(anywhere, anywhere, vmem, vmem),
        scratch_shapes=[
            pltpu.VMEM((FROWS, WIDTH), f32),
            pltpu.VMEM((WIDTH, QCOLS), bf16),
            pltpu.VMEM((N_ROWS, WIDTH), bf16),
            pltpu.VMEM((WIDTH, N_ROWS), bf16),
            pltpu.VMEM((NZ, WIDTH, QCOLS), bf16),
            pltpu.VMEM((NZ, QCOLS, WIDTH), bf16),
            pltpu.VMEM((NZ, N_ROWS, QCOLS), bf16),
            pltpu.VMEM((NZ, QCOLS, N_ROWS), bf16),
            pltpu.VMEM((NZ, QCOLS, N_ROWS), bf16),
            pltpu.VMEM((3, 8, QCOLS), f32),
            pltpu.VMEM((ITERS, NZ, 8, 128), f32),
            pltpu.VMEM((ITERS, NZ, NZ, 8, 128), f32),
            pltpu.VMEM((16, 128), f32),
            pltpu.VMEM((NP - 1, 16, 128), f32),
            pltpu.VMEM((ITERS - 1, 16, 128), bf16),
            pltpu.VMEM((ITERS - 1, NP - 1, 16, 128), bf16),
            dma((2,)), dma((4,)), dma((4,)), dma((4,)), dma((4,)), dma((4,)), dma((4,)),
            dma((15,)), dma((15,)), dma((16,)), dma((16,)),
            dma((ITERS, NZ)), dma((ITERS, NZ)), pltpu.SemaphoreType.DMA, pltpu.SemaphoreType.DMA, dma((ITERS - 1,)), dma((ITERS - 1,)),
            dma((2,)), pltpu.SemaphoreType.REGULAR,
        ],
        compiler_params=pltpu.CompilerParams(
            collective_id=0, has_side_effects=True, vmem_limit_bytes=44 * 2**20
        ),
        cost_estimate=pl.CostEstimate(
            flops=6 * N_ROWS * N_COLS * WIDTH, bytes_accessed=4 * 2**20, transcendentals=3 * N_ROWS * N_COLS
        ),
        name="balance",
    )(*(pltpu.with_memory_space_constraint(a, pltpu.HBM) for a in (features, prototypes)))


def write_kernel(f, p, r, c, out, buf, rc, sem):
    steps = N_ROWS // BLOCK
    turned = [jnp.broadcast_to(r[h, i:i + 1, :], (8, 128)).T[:, 0:1] for h in range(HALVES) for i in range(TILES)]
    rc[...] = jnp.concatenate(turned, axis=0)
    scale = [
        jnp.concatenate([c[q, i:i + 1, :] * float(ROWS * PROTOS) for i in range(QCOLS // 128)], axis=1)
        for q in range(NZ)
    ]

    def store(i):
        return pltpu.make_async_copy(
            buf.at[i], out.at[pl.ds(pl.multiple_of(i * BLOCK, BLOCK), BLOCK), :], sem.at[i]
        )

    def visit(i, carry):
        rows = pl.ds(pl.multiple_of(i * BLOCK, BLOCK), BLOCK)
        for q in range(NZ):
            s = jnp.dot(f[rows, :], p[q], preferred_element_type=jnp.float32)
            buf[i, :, q * QCOLS:(q + 1) * QCOLS] = jnp.exp2(s * EXP2_SCALE) * rc[rows, :] * scale[q]
        store(i).start()
        return carry

    lax.fori_loop(0, steps, visit, 0)
    for i in range(steps):
        store(i).wait()


def write(f, p, r, c):
    vmem = pl.BlockSpec(memory_space=pltpu.VMEM)
    return pl.pallas_call(
        write_kernel,
        out_shape=jax.ShapeDtypeStruct((N_ROWS, N_COLS), jnp.float32),
        in_specs=[vmem] * 4,
        out_specs=pl.BlockSpec(memory_space=pl.ANY),
        scratch_shapes=[
            pltpu.VMEM((N_ROWS // BLOCK, BLOCK, N_COLS), jnp.float32),
            pltpu.VMEM((N_ROWS, 1), jnp.float32),
            pltpu.SemaphoreType.DMA((N_ROWS // BLOCK,)),
        ],
        compiler_params=pltpu.CompilerParams(vmem_limit_bytes=40 * 2**20),
        cost_estimate=pl.CostEstimate(
            flops=2 * N_ROWS * N_COLS * WIDTH, bytes_accessed=18 * 2**20, transcendentals=N_ROWS * N_COLS
        ),
        name="write",
    )(f, p, r, c)


def body(features, prototypes):
    return write(*balance(features, prototypes))


def solution(mesh):
    in_specs = (P(("batch", "proto"), None), P(None, ("proto", "batch")))
    out_specs = P("batch", "proto")
    return jax.shard_map(body, mesh=mesh, in_specs=in_specs, out_specs=out_specs, check_vma=False)
```

```python
import functools

import jax
import jax.numpy as jnp
from jax import lax
from jax.experimental import pallas as pl
from jax.experimental.pallas import tpu as pltpu
from jax.sharding import PartitionSpec as P

ITERS = 3
PROTOS = 65536
ROWS = 8192
eps = 1e-06
sharpening_divisor = 0.07
LOG2E = 1.4426950408889634
EXP2_SCALE = LOG2E / sharpening_divisor

NZ = 4
NP = 32
N_ROWS = ROWS // NZ
N_COLS = PROTOS // NP
WIDTH = 256
QCOLS = N_COLS // NZ
FROWS = N_ROWS // NP
BLOCK = 256
HALVES = 2
HALF = N_ROWS // HALVES
TILES = HALF // 128
PCHUNK = WIDTH // 4
SLAB = N_ROWS // 4

MESH = pl.DeviceIdType.MESH


def hops(d):
    return sum(min(v, 4 - v) for v in d[:2])


CHIPS = sorted(((dx, dy) for dx in range(4) for dy in range(4) if dx or dy), key=hops, reverse=True)
PEERS = sorted(
    ((dx, dy, dc) for dx in range(4) for dy in range(4) for dc in range(2) if dx or dy or dc),
    key=hops, reverse=True,
)
NEAR = [(2, 0, 0), (0, 2, 0), (1, 0, 0), (3, 0, 0), (0, 1, 0), (0, 3, 0), (0, 0, 1)]


def operand(dense):
    high = dense.astype(jnp.bfloat16).astype(jnp.float32)
    low = dense - high
    tiles = [
        jnp.concatenate(
            [jnp.broadcast_to(high[i:i + 1], (8, 128)), jnp.broadcast_to(low[i:i + 1], (8, 128))], axis=0
        ).astype(jnp.bfloat16)
        for i in range(dense.shape[0])
    ]
    return jnp.concatenate(tiles, axis=1)


def matvec(parts, matrix):
    return jnp.dot(parts, matrix, preferred_element_type=jnp.float32)


def dense_rows(wide):
    row = lax.broadcasted_iota(jnp.int32, (8, 128), 0)
    out = wide[:, 0:128]
    for i in range(1, wide.shape[1] // 128):
        out = jnp.where(row == i, wide[:, i * 128:(i + 1) * 128], out)
    return out


def join(product):
    return dense_rows(product[0:8] + product[8:16])


def balance_kernel(
    feat_hbm, proto_hbm, f_out, p_out, r_out, c_out,
    feat, proto, fb, ft, pb, pt, e, et, el, col, zs, zr, ps, pr, qs, qr,
    s_in, s_right, s_left, s_fwd, r_left, r_right, r_far,
    s_feat, r_feat, s_sib, r_sib, s_z, r_z, s_p, r_p, s_q, r_q, s_out, greeted,
):
    z = lax.axis_index("batch")
    p = lax.axis_index("proto")
    x, y, core = p // 8, (p // 2) % 4, p % 2
    at_x = [((x + d) % 4) * 8 for d in range(4)]
    at_y = [((y + d) % 4) * 2 for d in range(4)]
    at_core = [core, 1 - core]
    at_z = [(z + d) % 4 for d in range(4)]
    right, far, left = at_z[1], at_z[2], at_z[3]

    def plane(dx, dy, dc):
        return at_x[dx % 4] + at_y[dy % 4] + at_core[dc]

    barrier = pltpu.get_barrier_semaphore()
    for dz in (2, 1, 3):
        pl.semaphore_signal(barrier, inc=1, device_id=(at_z[dz], p), device_id_type=MESH)
    for d in NEAR:
        pl.semaphore_signal(barrier, inc=1, device_id=(z, plane(*d)), device_id_type=MESH)

    proto_in = pltpu.make_async_copy(proto_hbm, proto, s_in.at[0])
    feat_in = pltpu.make_async_copy(feat_hbm, feat, s_in.at[1])
    proto_in.start()
    feat_in.start()

    def rows_of(owner):
        return pl.ds(pl.multiple_of(owner * FROWS, FROWS), FROWS)

    proto_in.wait()
    raw = proto[...].astype(jnp.float32)
    pb[z] = (raw * lax.rsqrt(jnp.sum(raw * raw, axis=0, keepdims=True) + eps)).astype(jnp.bfloat16)

    pl.semaphore_wait(barrier, NZ - 1 + len(NEAR))

    def send(src, dst, send_sem, recv_sem, target):
        pltpu.make_async_remote_copy(
            src_ref=src, dst_ref=dst, send_sem=send_sem, recv_sem=recv_sem,
            device_id=target, device_id_type=MESH,
        ).start()

    def arrived(ref, sem):
        pltpu.make_async_remote_copy(
            src_ref=ref, dst_ref=ref, send_sem=sem, recv_sem=sem,
            device_id=(right, p), device_id_type=MESH,
        ).wait_recv()

    def sent(ref, sem):
        pltpu.make_async_remote_copy(
            src_ref=ref, dst_ref=ref, send_sem=sem, recv_sem=sem,
            device_id=(right, p), device_id_type=MESH,
        ).wait_send()

    def chunk(owner, k):
        return pb.at[owner, pl.ds(k * PCHUNK, PCHUNK), :]

    for dx in (2, 1, 3):
        pl.semaphore_signal(greeted, inc=1, device_id=(z, plane(dx, 0, 0)), device_id_type=MESH)

    for k in range(4):
        kr, kl = k, (k + 2) % 4
        send(chunk(z, kr), chunk(z, kr), s_right.at[kr], r_left.at[kr], (right, p))
        send(chunk(z, kl), chunk(z, kl), s_left.at[kl], r_right.at[kl], (left, p))

    feat_in.wait()
    raw = feat[...]
    fb[rows_of(p), :] = (
        raw * lax.rsqrt(jnp.sum(raw * raw, axis=1, keepdims=True) + eps)
    ).astype(jnp.bfloat16)

    sibling = plane(0, 0, 1)
    mine = fb.at[rows_of(p), :]
    def send_features(slabs):
        for n, (dx, dy) in enumerate(CHIPS):
            if dx in slabs:
                send(mine, mine, s_feat.at[n], r_feat.at[n], (z, plane(dx, dy, 0)))

    send_features((0,))
    send(mine, mine, s_sib.at[15], r_sib.at[15], (z, sibling))
    pl.semaphore_wait(greeted, 3)
    send_features((1, 2, 3))

    def pass_features(slab):
        for n, (dx, dy) in enumerate(CHIPS):
            if dx == slab:
                block = fb.at[rows_of(plane(4 - dx, 4 - dy, 0)), :]
                arrived(block, r_feat.at[n])
                send(block, block, s_sib.at[n], r_sib.at[n], (z, sibling))

    def pass_proto(k):
        arrived(chunk(left, k), r_left.at[k])
        send(chunk(left, k), chunk(left, k), s_fwd.at[k], r_far.at[k], (right, p))
        arrived(chunk(right, k + 2), r_right.at[k + 2])
        send(chunk(right, k + 2), chunk(right, k + 2), s_fwd.at[k + 2], r_far.at[k + 2], (left, p))

    def wait_slab(slab):
        for n, (dx, dy) in enumerate(CHIPS):
            if dx == slab:
                arrived(fb.at[rows_of(plane(4 - dx, 4 - dy, 1)), :], r_sib.at[n])
        if slab == 0:
            arrived(fb.at[rows_of(sibling), :], r_sib.at[15])

    def send_columns(it, q):
        for dz in (2, 1, 3):
            send(zs.at[it, q], zr.at[it, q, dz], s_z.at[it, q], r_z.at[it, q], (at_z[dz], p))

    def score_rows(q, start, count):
        rows = pl.ds(pl.multiple_of(start, count), count)
        s = jnp.dot(fb[rows, :], pb[q], preferred_element_type=jnp.float32)
        t = jnp.exp2(s * EXP2_SCALE)
        e[q, rows, :] = t.astype(jnp.bfloat16)
        return jnp.sum(t.reshape(count // 8, 8, QCOLS), axis=0)

    def score_slab(q, slab):
        return score_rows(q, at_x[(4 - slab) % 4] * (SLAB // 8), SLAB)

    def finish_block(q, total):
        total = jnp.sum(total, axis=0, keepdims=True)
        zs[0, q] = dense_rows(jnp.broadcast_to(total, (8, QCOLS)))
        send_columns(0, q)

    def turn_features():
        ft[...] = fb[...].T

    def score_turned(q, low):
        if not low:
            pt[q] = pb[q].T

        s = jnp.dot(pt[q], ft[...], preferred_element_type=jnp.float32)
        t = jnp.exp2(s * EXP2_SCALE)
        high = t.astype(jnp.bfloat16)
        if low:
            el[q] = (t - high.astype(jnp.float32)).astype(jnp.bfloat16)
        else:
            et[q] = high

    pass_features(0)
    pass_proto(0)
    pass_features(1)
    pass_proto(1)
    pass_features(3)
    wait_slab(0)
    col[0] = score_slab(z, 0)
    wait_slab(1)
    col[0] += score_slab(z, 1)
    pass_features(2)
    wait_slab(3)
    col[0] += score_slab(z, 3)
    for k in (2, 3):
        arrived(chunk(left, k), r_left.at[k])
    for k in (0, 1):
        arrived(chunk(right, k), r_right.at[k])
    for i, q in ((1, left), (2, right)):
        col[i] = score_slab(q, 0) + score_slab(q, 1) + score_slab(q, 3)
    wait_slab(2)
    for i, q in enumerate((z, left, right)):
        finish_block(q, col[i] + score_slab(q, 2))
    for k in range(4):
        arrived(chunk(far, k), r_far.at[k])
    finish_block(far, score_rows(far, 0, N_ROWS))

    f_copy = pltpu.make_async_copy(fb, f_out, s_out.at[0])
    p_copy = pltpu.make_async_copy(pb, p_out, s_out.at[1])
    f_copy.start()
    p_copy.start()
    turn_features()
    for q in (z, left, right, far):
        score_turned(q, False)

    for it in range(ITERS):
        last = it == ITERS - 1
        if it > 0:
            arrived(qr.at[it - 1], r_q.at[it - 1])
            row_sum = qs[it - 1].astype(jnp.float32) + jnp.sum(qr[it - 1].astype(jnp.float32), axis=0)
            parts = operand(1.0 / (ROWS * row_sum))
            for q in range(NZ):
                zs[it, q] = join(matvec(parts, e[q]))
                send_columns(it, q)
        totals = [jnp.zeros((16, HALF), jnp.float32)] * HALVES
        for q in range(NZ):
            arrived(zr.at[it, q, pl.ds(1, NZ - 1)], r_z.at[it, q])
            col_scale = 1.0 / (PROTOS * (zs[it, q] + jnp.sum(zr[it, q, 1:NZ], axis=0)))
            if last:
                c_out[q] = col_scale
            parts = operand(col_scale[0:QCOLS // 128])
            for h in range(HALVES):
                rows = slice(h * HALF, (h + 1) * HALF)
                totals[h] = totals[h] + matvec(parts, et[q, :, rows])
                if last:
                    totals[h] = totals[h] + matvec(parts, el[q, :, rows])
                if last and q == NZ - 1:
                    ps[h * 8:(h + 1) * 8, :] = join(totals[h])
        if last:
            for j, d in enumerate(PEERS):
                send(ps, pr.at[j], s_p, r_p, (z, plane(*d)))
        if not last:
            qs[it] = jnp.concatenate([join(t) for t in totals], axis=0).astype(jnp.bfloat16)
            for j, d in enumerate(PEERS):
                send(qs.at[it], qr.at[it, j], s_q.at[it], r_q.at[it], (z, plane(*d)))
        if it == 0:
            for q in range(NZ):
                score_turned(q, True)

    for k in range(4):
        sent(chunk(z, k), s_right.at[k])
        sent(chunk(z, k), s_left.at[k])
        sent(chunk(z, k), s_fwd.at[k])
    for n in range(15):
        sent(mine, s_feat.at[n])
        sent(mine, s_sib.at[n])
    sent(mine, s_sib.at[15])
    for it in range(ITERS):
        for q in range(NZ):
            sent(zr.at[it, q, pl.ds(1, NZ - 1)], s_z.at[it, q])
    for it in range(ITERS - 1):
        sent(qr.at[it], s_q.at[it])
    f_copy.wait()
    p_copy.wait()

    arrived(pr, r_p)
    scale = 1.0 / (ROWS * (ps[...] + jnp.sum(pr[...], axis=0)))
    for h in range(HALVES):
        r_out[h] = scale[h * 8:(h + 1) * 8]

    sent(pr, s_p)


def balance(features, prototypes):
    f32, bf16 = jnp.float32, jnp.bfloat16
    vmem = pl.BlockSpec(memory_space=pltpu.VMEM)
    anywhere = pl.BlockSpec(memory_space=pl.ANY)
    hbm = pl.BlockSpec(memory_space=pltpu.HBM)
    dma = pltpu.SemaphoreType.DMA
    return pl.pallas_call(
        balance_kernel,
        out_shape=(
            jax.ShapeDtypeStruct((N_ROWS, WIDTH), bf16),
            jax.ShapeDtypeStruct((NZ, WIDTH, QCOLS), bf16),
            jax.ShapeDtypeStruct((HALVES, 8, 128), f32),
            jax.ShapeDtypeStruct((NZ, 8, 128), f32),
        ),
        in_specs=[hbm, hbm],
        out_specs=(anywhere, anywhere, vmem, vmem),
        scratch_shapes=[
            pltpu.VMEM((FROWS, WIDTH), f32),
            pltpu.VMEM((WIDTH, QCOLS), bf16),
            pltpu.VMEM((N_ROWS, WIDTH), bf16),
            pltpu.VMEM((WIDTH, N_ROWS), bf16),
            pltpu.VMEM((NZ, WIDTH, QCOLS), bf16),
            pltpu.VMEM((NZ, QCOLS, WIDTH), bf16),
            pltpu.VMEM((NZ, N_ROWS, QCOLS), bf16),
            pltpu.VMEM((NZ, QCOLS, N_ROWS), bf16),
            pltpu.VMEM((NZ, QCOLS, N_ROWS), bf16),
            pltpu.VMEM((3, 8, QCOLS), f32),
            pltpu.VMEM((ITERS, NZ, 8, 128), f32),
            pltpu.VMEM((ITERS, NZ, NZ, 8, 128), f32),
            pltpu.VMEM((16, 128), f32),
            pltpu.VMEM((NP - 1, 16, 128), f32),
            pltpu.VMEM((ITERS - 1, 16, 128), bf16),
            pltpu.VMEM((ITERS - 1, NP - 1, 16, 128), bf16),
            dma((2,)), dma((4,)), dma((4,)), dma((4,)), dma((4,)), dma((4,)), dma((4,)),
            dma((15,)), dma((15,)), dma((16,)), dma((16,)),
            dma((ITERS, NZ)), dma((ITERS, NZ)), pltpu.SemaphoreType.DMA, pltpu.SemaphoreType.DMA, dma((ITERS - 1,)), dma((ITERS - 1,)),
            dma((2,)), pltpu.SemaphoreType.REGULAR,
        ],
        compiler_params=pltpu.CompilerParams(
            collective_id=0, has_side_effects=True, vmem_limit_bytes=44 * 2**20
        ),
        cost_estimate=pl.CostEstimate(
            flops=6 * N_ROWS * N_COLS * WIDTH, bytes_accessed=4 * 2**20, transcendentals=3 * N_ROWS * N_COLS
        ),
        name="balance",
    )(*(pltpu.with_memory_space_constraint(a, pltpu.HBM) for a in (features, prototypes)))


def write_kernel(f, p, r, c, out, buf, rc, sem):
    steps = N_ROWS // BLOCK
    turned = [jnp.broadcast_to(r[h, i:i + 1, :], (8, 128)).T[:, 0:1] for h in range(HALVES) for i in range(TILES)]
    rc[...] = jnp.concatenate(turned, axis=0)
    scale = [
        jnp.concatenate([c[q, i:i + 1, :] * float(ROWS * PROTOS) for i in range(QCOLS // 128)], axis=1)
        for q in range(NZ)
    ]

    def store(i):
        return pltpu.make_async_copy(
            buf.at[i], out.at[pl.ds(pl.multiple_of(i * BLOCK, BLOCK), BLOCK), :], sem.at[i]
        )

    def visit(i, carry):
        rows = pl.ds(pl.multiple_of(i * BLOCK, BLOCK), BLOCK)
        for q in range(NZ):
            s = jnp.dot(f[rows, :], p[q], preferred_element_type=jnp.float32)
            buf[i, :, q * QCOLS:(q + 1) * QCOLS] = jnp.exp2(s * EXP2_SCALE) * rc[rows, :] * scale[q]
        store(i).start()
        return carry

    lax.fori_loop(0, steps, visit, 0)
    for i in range(steps):
        store(i).wait()


def write(f, p, r, c):
    vmem = pl.BlockSpec(memory_space=pltpu.VMEM)
    return pl.pallas_call(
        write_kernel,
        out_shape=jax.ShapeDtypeStruct((N_ROWS, N_COLS), jnp.float32),
        in_specs=[vmem] * 4,
        out_specs=pl.BlockSpec(memory_space=pl.ANY),
        scratch_shapes=[
            pltpu.VMEM((N_ROWS // BLOCK, BLOCK, N_COLS), jnp.float32),
            pltpu.VMEM((N_ROWS, 1), jnp.float32),
            pltpu.SemaphoreType.DMA((N_ROWS // BLOCK,)),
        ],
        compiler_params=pltpu.CompilerParams(vmem_limit_bytes=40 * 2**20),
        cost_estimate=pl.CostEstimate(
            flops=2 * N_ROWS * N_COLS * WIDTH, bytes_accessed=18 * 2**20, transcendentals=N_ROWS * N_COLS
        ),
        name="write",
    )(f, p, r, c)


def body(features, prototypes):
    return write(*balance(features, prototypes))


def solution(mesh):
    in_specs = (P(("batch", "proto"), None), P(None, ("proto", "batch")))
    out_specs = P("batch", "proto")
    return jax.shard_map(body, mesh=mesh, in_specs=in_specs, out_specs=out_specs, check_vma=False)
```

```python
import functools

import jax
import jax.numpy as jnp
from jax import lax
from jax.experimental import pallas as pl
from jax.experimental.pallas import tpu as pltpu
from jax.sharding import PartitionSpec as P

ITERS = 3
PROTOS = 65536
ROWS = 8192
eps = 1e-06
sharpening_divisor = 0.07
LOG2E = 1.4426950408889634
EXP2_SCALE = LOG2E / sharpening_divisor

NZ = 4
NP = 32
N_ROWS = ROWS // NZ
N_COLS = PROTOS // NP
WIDTH = 256
QCOLS = N_COLS // NZ
FROWS = N_ROWS // NP
WRITE_ROWS = (128, 128) + (256,) * 7
HALVES = 2
HALF = N_ROWS // HALVES
TILES = HALF // 128
PCHUNK = WIDTH // 4
SLAB = N_ROWS // 4

MESH = pl.DeviceIdType.MESH


def hops(d):
    return sum(min(v, 4 - v) for v in d[:2])


CHIPS = sorted(((dx, dy) for dx in range(4) for dy in range(4) if dx or dy), key=hops, reverse=True)
PEERS = sorted(
    ((dx, dy, dc) for dx in range(4) for dy in range(4) for dc in range(2) if dx or dy or dc),
    key=hops, reverse=True,
)
NEAR = [(2, 0, 0), (0, 2, 0), (1, 0, 0), (3, 0, 0), (0, 1, 0), (0, 3, 0), (0, 0, 1)]


def operand(dense):
    high = dense.astype(jnp.bfloat16).astype(jnp.float32)
    low = dense - high
    tiles = [
        jnp.concatenate(
            [jnp.broadcast_to(high[i:i + 1], (8, 128)), jnp.broadcast_to(low[i:i + 1], (8, 128))], axis=0
        ).astype(jnp.bfloat16)
        for i in range(dense.shape[0])
    ]
    return jnp.concatenate(tiles, axis=1)


def matvec(parts, matrix):
    return jnp.dot(parts, matrix, preferred_element_type=jnp.float32)


def dense_rows(wide):
    row = lax.broadcasted_iota(jnp.int32, (8, 128), 0)
    out = wide[:, 0:128]
    for i in range(1, wide.shape[1] // 128):
        out = jnp.where(row == i, wide[:, i * 128:(i + 1) * 128], out)
    return out


def join(product):
    return dense_rows(product[0:8] + product[8:16])


def balance_kernel(
    feat_hbm, proto_hbm, f_out, p_out, r_out, c_out,
    feat, proto, fb, ft, pb, pt, e, et, el, col, zs, zr, ps, pr, qs, qr,
    s_in, s_right, s_left, s_fwd, r_left, r_right, r_far,
    s_feat, r_feat, s_sib, r_sib, s_z, r_z, s_p, r_p, s_q, r_q, s_out, greeted,
):
    z = lax.axis_index("batch")
    p = lax.axis_index("proto")
    x, y, core = p // 8, (p // 2) % 4, p % 2
    at_x = [((x + d) % 4) * 8 for d in range(4)]
    at_y = [((y + d) % 4) * 2 for d in range(4)]
    at_core = [core, 1 - core]
    at_z = [(z + d) % 4 for d in range(4)]
    right, far, left = at_z[1], at_z[2], at_z[3]

    def plane(dx, dy, dc):
        return at_x[dx % 4] + at_y[dy % 4] + at_core[dc]

    barrier = pltpu.get_barrier_semaphore()
    for dz in (2, 1, 3):
        pl.semaphore_signal(barrier, inc=1, device_id=(at_z[dz], p), device_id_type=MESH)
    for d in NEAR:
        pl.semaphore_signal(barrier, inc=1, device_id=(z, plane(*d)), device_id_type=MESH)

    proto_in = pltpu.make_async_copy(proto_hbm, proto, s_in.at[0])
    feat_in = pltpu.make_async_copy(feat_hbm, feat, s_in.at[1])
    proto_in.start()
    feat_in.start()

    def rows_of(owner):
        return pl.ds(pl.multiple_of(owner * FROWS, FROWS), FROWS)

    proto_in.wait()
    raw = proto[...].astype(jnp.float32)
    pb[z] = (raw * lax.rsqrt(jnp.sum(raw * raw, axis=0, keepdims=True) + eps)).astype(jnp.bfloat16)
    feat_in.wait()
    raw = feat[...]
    fb[rows_of(p), :] = (
        raw * lax.rsqrt(jnp.sum(raw * raw, axis=1, keepdims=True) + eps)
    ).astype(jnp.bfloat16)

    pl.semaphore_wait(barrier, NZ - 1 + len(NEAR))

    def send(src, dst, send_sem, recv_sem, target):
        pltpu.make_async_remote_copy(
            src_ref=src, dst_ref=dst, send_sem=send_sem, recv_sem=recv_sem,
            device_id=target, device_id_type=MESH,
        ).start()

    def arrived(ref, sem):
        pltpu.make_async_remote_copy(
            src_ref=ref, dst_ref=ref, send_sem=sem, recv_sem=sem,
            device_id=(right, p), device_id_type=MESH,
        ).wait_recv()

    def sent(ref, sem):
        pltpu.make_async_remote_copy(
            src_ref=ref, dst_ref=ref, send_sem=sem, recv_sem=sem,
            device_id=(right, p), device_id_type=MESH,
        ).wait_send()

    def chunk(owner, k):
        return pb.at[owner, pl.ds(k * PCHUNK, PCHUNK), :]

    for k in range(4):
        kr, kl = k, (k + 2) % 4
        send(chunk(z, kr), chunk(z, kr), s_right.at[kr], r_left.at[kr], (right, p))
        send(chunk(z, kl), chunk(z, kl), s_left.at[kl], r_right.at[kl], (left, p))

    sibling = plane(0, 0, 1)
    mine = fb.at[rows_of(p), :]
    def send_features(slabs):
        for n, (dx, dy) in enumerate(CHIPS):
            if dx in slabs:
                send(mine, mine, s_feat.at[n], r_feat.at[n], (z, plane(dx, dy, 0)))

    for dx in (2, 1, 3):
        pl.semaphore_signal(greeted, inc=1, device_id=(z, plane(dx, 0, 0)), device_id_type=MESH)
    send_features((0,))
    send(mine, mine, s_sib.at[15], r_sib.at[15], (z, sibling))
    pl.semaphore_wait(greeted, 3)
    send_features((1, 2, 3))

    def pass_features(slab):
        for n, (dx, dy) in enumerate(CHIPS):
            if dx == slab:
                block = fb.at[rows_of(plane(4 - dx, 4 - dy, 0)), :]
                arrived(block, r_feat.at[n])
                send(block, block, s_sib.at[n], r_sib.at[n], (z, sibling))

    def pass_proto(k):
        arrived(chunk(left, k), r_left.at[k])
        send(chunk(left, k), chunk(left, k), s_fwd.at[k], r_far.at[k], (right, p))
        arrived(chunk(right, k + 2), r_right.at[k + 2])
        send(chunk(right, k + 2), chunk(right, k + 2), s_fwd.at[k + 2], r_far.at[k + 2], (left, p))

    def wait_slab(slab):
        for n, (dx, dy) in enumerate(CHIPS):
            if dx == slab:
                arrived(fb.at[rows_of(plane(4 - dx, 4 - dy, 1)), :], r_sib.at[n])
        if slab == 0:
            arrived(fb.at[rows_of(sibling), :], r_sib.at[15])

    def send_columns(it, q):
        for dz in (2, 1, 3):
            send(zs.at[it, q], zr.at[it, q, dz], s_z.at[it, q], r_z.at[it, q], (at_z[dz], p))

    def score_rows(q, start, count):
        rows = pl.ds(pl.multiple_of(start, count), count)
        s = jnp.dot(fb[rows, :], pb[q], preferred_element_type=jnp.float32)
        t = jnp.exp2(s * EXP2_SCALE)
        e[q, rows, :] = t.astype(jnp.bfloat16)
        return jnp.sum(t.reshape(count // 8, 8, QCOLS), axis=0)

    def score_slab(q, slab):
        return score_rows(q, at_x[(4 - slab) % 4] * (SLAB // 8), SLAB)

    def finish_block(q, total):
        total = jnp.sum(total, axis=0, keepdims=True)
        zs[0, q] = dense_rows(jnp.broadcast_to(total, (8, QCOLS)))
        send_columns(0, q)

    def turn_features():
        ft[...] = fb[...].T

    def score_turned(q, low):
        if not low:
            pt[q] = pb[q].T

        s = jnp.dot(pt[q], ft[...], preferred_element_type=jnp.float32)
        t = jnp.exp2(s * EXP2_SCALE)
        high = t.astype(jnp.bfloat16)
        if low:
            el[q] = (t - high.astype(jnp.float32)).astype(jnp.bfloat16)
        else:
            et[q] = high

    pass_features(0)
    pass_proto(0)
    pass_features(1)
    pass_proto(1)
    pass_features(3)
    wait_slab(0)
    col[0] = score_slab(z, 0)
    wait_slab(1)
    col[0] += score_slab(z, 1)
    pass_features(2)
    wait_slab(3)
    col[0] += score_slab(z, 3)
    for k in (2, 3):
        arrived(chunk(left, k), r_left.at[k])
    for k in (0, 1):
        arrived(chunk(right, k), r_right.at[k])
    for i, q in ((1, left), (2, right)):
        col[i] = score_slab(q, 0) + score_slab(q, 1) + score_slab(q, 3)
    wait_slab(2)
    for i, q in enumerate((z, left, right)):
        finish_block(q, col[i] + score_slab(q, 2))
    for k in range(4):
        arrived(chunk(far, k), r_far.at[k])
    finish_block(far, score_rows(far, 0, N_ROWS))

    f_copy = pltpu.make_async_copy(fb, f_out, s_out.at[0])
    p_copy = pltpu.make_async_copy(pb, p_out, s_out.at[1])
    f_copy.start()
    p_copy.start()
    turn_features()
    for q in (z, left, right, far):
        score_turned(q, False)

    for it in range(ITERS):
        last = it == ITERS - 1
        if it > 0:
            arrived(qr.at[it - 1], r_q.at[it - 1])
            row_sum = qs[it - 1].astype(jnp.float32) + jnp.sum(qr[it - 1].astype(jnp.float32), axis=0)
            parts = operand(1.0 / (ROWS * row_sum))
            for q in range(NZ):
                zs[it, q] = join(matvec(parts, e[q]))
                send_columns(it, q)
        totals = [jnp.zeros((16, HALF), jnp.float32)] * HALVES
        for q in range(NZ):
            arrived(zr.at[it, q, pl.ds(1, NZ - 1)], r_z.at[it, q])
            col_scale = 1.0 / (PROTOS * (zs[it, q] + jnp.sum(zr[it, q, 1:NZ], axis=0)))
            if last:
                c_out[q] = col_scale
            parts = operand(col_scale[0:QCOLS // 128])
            for h in range(HALVES):
                rows = slice(h * HALF, (h + 1) * HALF)
                totals[h] = totals[h] + matvec(parts, et[q, :, rows])
                if last:
                    totals[h] = totals[h] + matvec(parts, el[q, :, rows])
                if last and q == NZ - 1:
                    ps[h * 8:(h + 1) * 8, :] = join(totals[h])
        if last:
            for j, d in enumerate(PEERS):
                send(ps, pr.at[j], s_p, r_p, (z, plane(*d)))
        if not last:
            qs[it] = jnp.concatenate([join(t) for t in totals], axis=0).astype(jnp.bfloat16)
            for j, d in enumerate(PEERS):
                send(qs.at[it], qr.at[it, j], s_q.at[it], r_q.at[it], (z, plane(*d)))
        if it == 0:
            for q in range(NZ):
                score_turned(q, True)

    for k in range(4):
        sent(chunk(z, k), s_right.at[k])
        sent(chunk(z, k), s_left.at[k])
        sent(chunk(z, k), s_fwd.at[k])
    for n in range(15):
        sent(mine, s_feat.at[n])
        sent(mine, s_sib.at[n])
    sent(mine, s_sib.at[15])
    for it in range(ITERS):
        for q in range(NZ):
            sent(zr.at[it, q, pl.ds(1, NZ - 1)], s_z.at[it, q])
    for it in range(ITERS - 1):
        sent(qr.at[it], s_q.at[it])
    f_copy.wait()
    p_copy.wait()

    arrived(pr, r_p)
    scale = 1.0 / (ROWS * (ps[...] + jnp.sum(pr[...], axis=0)))
    for h in range(HALVES):
        r_out[h] = scale[h * 8:(h + 1) * 8]

    sent(pr, s_p)


def balance(features, prototypes):
    f32, bf16 = jnp.float32, jnp.bfloat16
    vmem = pl.BlockSpec(memory_space=pltpu.VMEM)
    anywhere = pl.BlockSpec(memory_space=pl.ANY)
    hbm = pl.BlockSpec(memory_space=pltpu.HBM)
    dma = pltpu.SemaphoreType.DMA
    return pl.pallas_call(
        balance_kernel,
        out_shape=(
            jax.ShapeDtypeStruct((N_ROWS, WIDTH), bf16),
            jax.ShapeDtypeStruct((NZ, WIDTH, QCOLS), bf16),
            jax.ShapeDtypeStruct((HALVES, 8, 128), f32),
            jax.ShapeDtypeStruct((NZ, 8, 128), f32),
        ),
        in_specs=[hbm, hbm],
        out_specs=(anywhere, anywhere, vmem, vmem),
        scratch_shapes=[
            pltpu.VMEM((FROWS, WIDTH), f32),
            pltpu.VMEM((WIDTH, QCOLS), bf16),
            pltpu.VMEM((N_ROWS, WIDTH), bf16),
            pltpu.VMEM((WIDTH, N_ROWS), bf16),
            pltpu.VMEM((NZ, WIDTH, QCOLS), bf16),
            pltpu.VMEM((NZ, QCOLS, WIDTH), bf16),
            pltpu.VMEM((NZ, N_ROWS, QCOLS), bf16),
            pltpu.VMEM((NZ, QCOLS, N_ROWS), bf16),
            pltpu.VMEM((NZ, QCOLS, N_ROWS), bf16),
            pltpu.VMEM((3, 8, QCOLS), f32),
            pltpu.VMEM((ITERS, NZ, 8, 128), f32),
            pltpu.VMEM((ITERS, NZ, NZ, 8, 128), f32),
            pltpu.VMEM((16, 128), f32),
            pltpu.VMEM((NP - 1, 16, 128), f32),
            pltpu.VMEM((ITERS - 1, 16, 128), bf16),
            pltpu.VMEM((ITERS - 1, NP - 1, 16, 128), bf16),
            dma((2,)), dma((4,)), dma((4,)), dma((4,)), dma((4,)), dma((4,)), dma((4,)),
            dma((15,)), dma((15,)), dma((16,)), dma((16,)),
            dma((ITERS, NZ)), dma((ITERS, NZ)), pltpu.SemaphoreType.DMA, pltpu.SemaphoreType.DMA, dma((ITERS - 1,)), dma((ITERS - 1,)),
            dma((2,)), pltpu.SemaphoreType.REGULAR,
        ],
        compiler_params=pltpu.CompilerParams(
            collective_id=0, has_side_effects=True, vmem_limit_bytes=44 * 2**20
        ),
        cost_estimate=pl.CostEstimate(
            flops=6 * N_ROWS * N_COLS * WIDTH, bytes_accessed=4 * 2**20, transcendentals=3 * N_ROWS * N_COLS
        ),
        name="balance",
    )(*(pltpu.with_memory_space_constraint(a, pltpu.HBM) for a in (features, prototypes)))


def write_kernel(f, p, r, c, out, buf, sem):
    scale = [
        jnp.concatenate([c[q, i:i + 1, :] * float(ROWS * PROTOS) for i in range(QCOLS // 128)], axis=1)
        for q in range(NZ)
    ]
    stores = []
    start = 0
    for n, count in enumerate(WRITE_ROWS):
        rows = slice(start, start + count)
        tiles = [divmod(i, TILES) for i in range(start // 128, (start + count) // 128)]
        row_scale = jnp.concatenate([jnp.broadcast_to(r[h, i:i + 1, :], (8, 128)).T[:, 0:1] for h, i in tiles], axis=0)
        for q in range(NZ):
            s = jnp.dot(f[rows, :], p[q], preferred_element_type=jnp.float32)
            buf[rows, q * QCOLS:(q + 1) * QCOLS] = jnp.exp2(s * EXP2_SCALE) * row_scale * scale[q]
        copy = pltpu.make_async_copy(buf.at[pl.ds(start, count), :], out.at[pl.ds(start, count), :], sem.at[n])
        copy.start()
        stores.append(copy)
        start += count
    for copy in stores:
        copy.wait()


def write(f, p, r, c):
    vmem = pl.BlockSpec(memory_space=pltpu.VMEM)
    return pl.pallas_call(
        write_kernel,
        out_shape=jax.ShapeDtypeStruct((N_ROWS, N_COLS), jnp.float32),
        in_specs=[vmem] * 4,
        out_specs=pl.BlockSpec(memory_space=pl.ANY),
        scratch_shapes=[
            pltpu.VMEM((N_ROWS, N_COLS), jnp.float32),
            pltpu.SemaphoreType.DMA((len(WRITE_ROWS),)),
        ],
        compiler_params=pltpu.CompilerParams(vmem_limit_bytes=40 * 2**20),
        cost_estimate=pl.CostEstimate(
            flops=2 * N_ROWS * N_COLS * WIDTH, bytes_accessed=18 * 2**20, transcendentals=N_ROWS * N_COLS
        ),
        name="write",
    )(f, p, r, c)


def body(features, prototypes):
    return write(*balance(features, prototypes))


def solution(mesh):
    in_specs = (P(("batch", "proto"), None), P(None, ("proto", "batch")))
    out_specs = P("batch", "proto")
    return jax.shard_map(body, mesh=mesh, in_specs=in_specs, out_specs=out_specs, check_vma=False)
```
